256 devices in a mesh: tm: 32 (over x, y, z_hi), mp: 8 (over z_lo, core).
Axes of the slice: x: 4, y: 4, z: 8 (z_hi: 2, z_lo: 4; z = z_hi * 4 + z_lo), core: 2. Of those that a mesh axis runs over, the one named last changes fastest.
Arguments:
- frames: bfloat16 [4, 20480, 1024], P(None, 'tm'), may hold values from -8 to 8
- valid: int32 [4], replicated, may hold values from 5120 to 20480, as said below
- ln1_gain: float32 [1024], replicated, may hold values from 0.5 to 4
- w_query: bfloat16 [1024, 1024], P(None, 'mp'), may hold values from -0.1875 to 0.1875
- w_key: bfloat16 [1024, 1024], P(None, 'mp'), may hold values from -0.1875 to 0.1875
- w_value: bfloat16 [1024, 1024], P(None, 'mp'), may hold values from -0.1875 to 0.1875
- w_out: bfloat16 [1024, 1024], P('mp'), may hold values from -0.1875 to 0.1875
- ln2_gain: float32 [1024], replicated, may hold values from 0.5 to 4
- w_up: bfloat16 [1024, 4096], P(None, 'mp'), may hold values from -0.1875 to 0.1875
- w_down: bfloat16 [4096, 1024], P('mp'), may hold values from -0.09375 to 0.09375
Outputs:
- layer_out: bfloat16 [4, 20480, 1024], P(None, 'tm', 'mp')
The draws below stay inside these ranges and needn't reach their ends.
Inputs may be any that keep to these rules, and one draw needn't show every extreme that they name: `valid`: live frames of each recording; recording 0 is complete.
All inputs are finite; a program needn't handle non-finite values.
Results may differ from the reference program's by a relative error of at most 0.027.
Values may be sent and summed in bfloat16 or wider, within the bound.
A program may use at most 128 MiB of HBM per device.

```python
import jax
import jax.numpy as jnp
from jax import lax

D = 1024
FF = 4096
HEADS = 16
HD = 64
SEG = 160
LOOK = 32
REC = 4
FRAMES = 20480
N_MP = 8


def draw_valid(key, part):
    key = jax.random.fold_in(key, 1)
    others = jax.random.randint(key, (REC - 1,), FRAMES // 4, FRAMES + 1, dtype=jnp.int32)
    return jnp.concatenate([jnp.full((1,), FRAMES, jnp.int32), others])


def draw_ln1_gain(key, part):
    key = jax.random.fold_in(key, 2)
    return jax.random.uniform(key, (D,), jnp.float32, 0.6, 1.4)


def draw_ln2_gain(key, part):
    key = jax.random.fold_in(key, 3)
    return jax.random.uniform(key, (D,), jnp.float32, 0.6, 1.4)


def draw_frames(key, part):
    key = jax.random.fold_in(key, 4)
    noise_key, segment_key, record_key = jax.random.split(key, 3)
    segments = FRAMES // SEG
    segment_part = jax.random.normal(segment_key, (REC, segments, 1, D), jnp.float32)
    record_part = jax.random.normal(record_key, (REC, 1, 1, D), jnp.float32)
    noise = jax.random.normal(noise_key, (REC, segments, SEG, D), jnp.float32)
    total = noise + 1.5 * segment_part + 0.3 * record_part
    return jnp.clip(total, -8.0, 8.0).reshape(REC, FRAMES, D).astype(jnp.bfloat16)


def steps_of(stream_key, shape, cuts, least, high):
    def one(dim, blocks):
        draws = jax.random.uniform(jax.random.fold_in(jax.random.fold_in(stream_key, 6), dim), (blocks,), jnp.float32, least / len(cuts), high / len(cuts))
        return jnp.repeat(jnp.exp(draws), shape[dim] // blocks).reshape((-1,) + (1,) * (len(shape) - dim - 1))

    loudness = one(*cuts[0])
    for cut in cuts[1:]:
        loudness = loudness * one(*cut)
    return loudness


def gaussian(stream_key, extent, scale, most, cuts=(), kind=jnp.bfloat16):
    values = scale * jax.random.normal(stream_key, extent, jnp.float32)
    if cuts:
        values = values * steps_of(stream_key, extent, cuts, -0.22, 0.18)
    return jnp.clip(values, -most, most).astype(kind)


def setup_inputs(seed: int = 0) -> dict:
    streams_of = jax.random.split(jax.random.key(seed), 11)
    return {
        "frames": draw_frames(jax.random.fold_in(streams_of[10], 71), 0),
        "valid": draw_valid(jax.random.fold_in(streams_of[10], 71), 0),
        "ln1_gain": draw_ln1_gain(jax.random.fold_in(streams_of[10], 71), 0),
        "w_query": gaussian(streams_of[3], (D, HEADS * HD), D ** -0.5, 0.1875, ((1, 8),)),
        "w_key": gaussian(streams_of[4], (D, HEADS * HD), D ** -0.5, 0.1875, ((1, 8),)),
        "w_value": gaussian(streams_of[5], (D, HEADS * HD), D ** -0.5, 0.1875, ((1, 8),)),
        "w_out": gaussian(streams_of[6], (HEADS * HD, D), (HEADS * HD) ** -0.5, 0.1875, ((0, 8),)),
        "ln2_gain": draw_ln2_gain(jax.random.fold_in(streams_of[10], 71), 0),
        "w_up": gaussian(streams_of[8], (D, FF), D ** -0.5, 0.1875, ((1, 8),)),
        "w_down": gaussian(streams_of[9], (FF, D), FF ** -0.5, 0.09375, ((0, 8),)),
    }


EPS = 1e-05
NEG = -1e+30

def normalize(source, gain):
    width = source.shape[-1]
    mean = lax.optimization_barrier(jnp.sum(source, -1, keepdims=True)) / width
    square = lax.optimization_barrier(jnp.sum(source * source, -1, keepdims=True)) / width
    return (source - mean) * lax.rsqrt(square - mean * mean + EPS) * gain

def ahead(extended, seg, look, count):
    tail = extended[:, seg:]
    padding = count * seg - tail.shape[1]
    filler = jnp.zeros((tail.shape[0], padding) + tail.shape[2:], tail.dtype)
    tail = jnp.concatenate([tail, filler], 1)
    return tail.reshape((tail.shape[0], count, seg) + tail.shape[2:])[:, :, :look]

def attend(query, keys, values, live, bank_keys, bank_values, bank_ok, scale):
    qf = query.astype(jnp.float32)
    local = jnp.einsum('bsqhe,bslhe->bsqhl', qf, keys.astype(jnp.float32)) * scale
    local = jnp.where(live[:, :, None, None, :], local, NEG)
    top = lax.optimization_barrier(jnp.max(local, -1, keepdims=True))
    if bank_keys is not None:
        far = jnp.einsum('bsqhe,bmhe->bsqhm', qf, bank_keys.astype(jnp.float32)) * scale
        far = jnp.where(bank_ok[:, :, None, None, :], far, NEG)
        top = jnp.maximum(top, lax.optimization_barrier(jnp.max(far, -1, keepdims=True)))
    near_p = jnp.exp(local - top)
    total = lax.optimization_barrier(jnp.sum(near_p, -1, keepdims=True))
    if bank_keys is not None:
        far_p = jnp.exp(far - top)
        total = total + lax.optimization_barrier(jnp.sum(far_p, -1, keepdims=True))
    near_w = (near_p / total).astype(jnp.bfloat16).astype(jnp.float32)
    result = jnp.einsum('bsqhl,bslhe->bsqhe', near_w, values.astype(jnp.float32))
    if bank_keys is not None:
        far_w = (far_p / total).astype(jnp.bfloat16).astype(jnp.float32)
        result = result + jnp.einsum('bsqhm,bmhe->bsqhe', far_w, bank_values.astype(jnp.float32))
    return result.astype(jnp.bfloat16)

def headwise(query, keys, values, live, bank_keys, bank_values, bank_ok, scale):
    pieces = []
    for head in range(query.shape[3]):
        pick = slice(head, head + 1)
        if bank_keys is None:
            pieces.append(attend(query[:, :, :, pick], keys[:, :, :, pick], values[:, :, :, pick], live, None, None, None, scale))
        else:
            pieces.append(attend(query[:, :, :, pick], keys[:, :, :, pick], values[:, :, :, pick], live, bank_keys[:, :, pick], bank_values[:, :, pick], bank_ok, scale))
    return jnp.concatenate(pieces, 3)

def grouped_project(left, weight, groups):
    share = left.shape[-1] // groups
    total = jnp.zeros(left.shape[:-1] + (weight.shape[1],), jnp.float32)
    for group in range(groups):
        part = jnp.dot(left[..., group * share:(group + 1) * share], weight[group * share:(group + 1) * share], preferred_element_type=jnp.float32)
        total = total + lax.optimization_barrier(part.astype(jnp.bfloat16)).astype(jnp.float32)
    return total

def reference(frames, valid, ln1_gain, w_query, w_key, w_value, w_out, ln2_gain, w_up, w_down):
    rec, span, width = frames.shape
    segs = span // SEG
    heads = w_query.shape[1] // HD
    scale = HD ** (-0.5)
    xf = frames.astype(jnp.float32)
    normed = normalize(xf, ln1_gain).astype(jnp.bfloat16)
    positions = jnp.arange(span, dtype=jnp.int32)
    live = positions[None, :] < valid[:, None]

    def project(rows, weight):
        return jnp.dot(rows, weight, preferred_element_type=jnp.float32).astype(jnp.bfloat16).reshape(rows.shape[:-1] + (heads, HD))
    query = project(normed, w_query)
    keys = project(normed, w_key)
    values = project(normed, w_value)
    pad_kv = jnp.zeros((rec, LOOK, heads, HD), jnp.bfloat16)
    pad_live = jnp.zeros((rec, LOOK), bool)
    keys_local = jnp.concatenate([keys.reshape(rec, segs, SEG, heads, HD), ahead(jnp.concatenate([keys, pad_kv], 1), SEG, LOOK, segs)], 2)
    values_local = jnp.concatenate([values.reshape(rec, segs, SEG, heads, HD), ahead(jnp.concatenate([values, pad_kv], 1), SEG, LOOK, segs)], 2)
    live_local = jnp.concatenate([live.reshape(rec, segs, SEG), ahead(jnp.concatenate([live, pad_live], 1), SEG, LOOK, segs)], 2)
    seg_ids = jnp.arange(segs, dtype=jnp.int32)
    counts = jnp.clip(valid[:, None] - seg_ids[None, :] * SEG, 0, SEG).astype(jnp.int32)
    masked = normed.astype(jnp.float32).reshape(rec, segs, SEG, width) * live.reshape(rec, segs, SEG)[..., None].astype(jnp.float32)
    summary = (lax.optimization_barrier(jnp.sum(masked, 2)) / jnp.maximum(counts, 1)[..., None].astype(jnp.float32)).astype(jnp.bfloat16)
    sum_query = project(summary, w_query)[:, :, None]
    sum_out = headwise(sum_query, keys_local, values_local, live_local, None, None, None, scale).reshape(rec, segs, heads * HD)
    memory = grouped_project(sum_out, w_out, N_MP).astype(jnp.bfloat16)
    bank_keys = project(memory, w_key)
    bank_values = project(memory, w_value)
    bank_ok = (seg_ids[None, None, :] < seg_ids[None, :, None]) & (counts[:, None, :] > 0)
    frame_out = headwise(query.reshape(rec, segs, SEG, heads, HD), keys_local, values_local, live_local, bank_keys, bank_values, bank_ok, scale).reshape(rec, span, heads * HD)
    mixed = xf + grouped_project(frame_out, w_out, N_MP)
    normed_two = normalize(mixed, ln2_gain).astype(jnp.bfloat16)
    hidden = jax.nn.gelu(jnp.dot(normed_two, w_up, preferred_element_type=jnp.float32), approximate=False).astype(jnp.bfloat16)
    return (mixed + grouped_project(hidden, w_down, N_MP)).astype(jnp.bfloat16)
```

```python
import jax
import jax.numpy as jnp
from jax import lax
from jax.experimental import pallas as pl
from jax.experimental.pallas import tpu as pltpu
from jax.sharding import PartitionSpec as P

MESH = pl.DeviceIdType.MESH
F32 = jnp.float32
BF16 = jnp.bfloat16

D = 1024
SEG = 160
LOOK = 32
KEYS = SEG + LOOK
OWN = 2 * SEG
ROWS = OWN + LOOK
EXT = ROWS + 16
SLOTS = 128
EPS = 1e-05
NEG = -1e30
N_SEM = 208


def dot(a, b):
    return jnp.dot(a, b, preferred_element_type=F32)


def dot_t(a, b):
    return lax.dot_general(a, b, (((1,), (1,)), ((), ())), preferred_element_type=F32)


def normalize(x, gain):
    mean = jnp.sum(x, -1, keepdims=True) * (1.0 / D)
    square = jnp.sum(x * x, -1, keepdims=True) * (1.0 / D)
    return (x - mean) * lax.rsqrt(square - mean * mean + EPS) * gain


def kernel(
    valid, g1, g2, frames, wq, wk, wv, wo, up, dn, out,
    xs, nrm, qb, kb, vb, wq_b, wk_b, wv_b, wo_b, up_b, dn_b,
    mrow, mem_b, memf, bk, bv, fo, mixed, n2, hid, ob,
    loc_sem, send_sem, recv_sem,
):
    tm = lax.axis_index("tm")
    mp = lax.axis_index("mp")
    x = tm // 8
    y = (tm // 2) % 4
    zl = mp // 2
    z = (tm % 2) * 4 + zl
    c = mp % 2
    rec = zl

    def dev(px, py, pz, pc):
        return ((px * 4 + py) * 2 + pz // 4, (pz % 4) * 2 + pc)

    def z_dev(step):
        return dev(x, y, (z + step + 8) % 8, c)

    sibling = (tm, zl * 2 + 1 - c)

    used = [0]
    sent = []

    def remote(src, dst, to):
        i = used[0]
        used[0] += 1
        copy = pltpu.make_async_remote_copy(
            src_ref=src, dst_ref=dst, send_sem=send_sem.at[i], recv_sem=recv_sem.at[i],
            device_id=to, device_id_type=MESH,
        )
        sent.append(copy)
        copy.start()
        return copy

    n_local = [0]

    def local(src, dst):
        i = n_local[0]
        n_local[0] += 1
        copy = pltpu.make_async_copy(src, dst, loc_sem.at[i])
        copy.start()
        return copy

    xs_copy = local(frames.at[rec, pl.ds(c * OWN, OWN), :], xs.at[pl.ds(0, OWN)])
    own_copies = [
        local(wq, wq_b.at[0, 0]), local(wk, wk_b.at[0, 0]), local(wv, wv_b.at[0, 0]),
        local(wo, wo_b.at[0, 0]),
    ]
    for j in range(2):
        own_copies.append(local(up.at[:, pl.ds(j * 256, 256)], up_b.at[j, 0, 0]))

    def q_cols(step):
        return pl.ds(pl.multiple_of(((zl + step) % 4) * 256, 256), 256)

    for r in range(4):
        own_copies.append(local(dn.at[:, q_cols(r)], dn_b.at[r, 0, 0]))

    look_sem = n_local[0]
    n_local[0] += 1

    @pl.when(c == 0)
    def _():
        pltpu.make_async_copy(
            frames.at[rec, pl.ds(OWN, LOOK), :], xs.at[pl.ds(OWN, LOOK)], loc_sem.at[look_sem]
        ).start()

    barrier = pltpu.get_barrier_semaphore()

    def greet(i, carry):
        pl.semaphore_signal(barrier, inc=1, device_id=((tm + i) % 32, mp), device_id_type=MESH)
        return carry

    lax.fori_loop(1, 32, greet, 0)

    def greet_mp(i, carry):
        pl.semaphore_signal(barrier, inc=1, device_id=(tm, (mp + i) % 8), device_id_type=MESH)
        return carry

    lax.fori_loop(1, 8, greet_mp, 0)
    for step in (1, -1, 2, -2):
        pl.semaphore_signal(barrier, inc=1, device_id=z_dev(step), device_id_type=MESH)
    pl.semaphore_wait(barrier, 31 + 7 + 4)

    lx = (x + c) % 4
    ly = (y + c) % 4

    def at_x(label):
        return dev((label + 4 - c) % 4, y, z, c)

    def at_y(label):
        return dev(x, (label + 4 - c) % 4, z, c)

    def first(label):
        return label + 1 - 2 * (label % 2)

    def second(label):
        return 3 - label

    events = []

    class Half:
        def __init__(self, kind, source, view, base, rows):
            self.source, self.view, self.base, self.rows = source, view, base, rows
            if kind == 0:
                self.a, self.b, self.at_a, self.at_b = lx, ly, at_x, at_y
            else:
                self.a, self.b, self.at_a, self.at_b = ly, lx, at_y, at_x
            self.far = 2 if kind == 0 else -2

        def span(self, index, count):
            return pl.ds(pl.multiple_of(self.base + index * self.rows, self.rows), count * self.rows)

        def z(self):
            here = self.span(self.b * 4 + self.a, 1)
            self.arrive = [
                remote(self.source(1, here), self.view(0, pl.ds(3, 1), here), z_dev(1)),
                remote(self.source(-1, here), self.view(0, pl.ds(1, 1), here), z_dev(-1)),
                remote(self.source(self.far, here), self.view(0, pl.ds(2, 1), here), z_dev(self.far)),
            ]

        def hop(self, rows, to):
            for copy in self.arrive:
                copy.wait_recv()
            part = self.view(0, pl.ds(1, 3), rows)
            self.arrive = [remote(part, part, to)]

        def s1(self):
            self.hop(self.span(self.b * 4 + self.a, 1), self.at_a(first(self.a)))

        def s2(self):
            self.hop(self.span(self.b * 4 + 2 * (self.a // 2), 2), self.at_a(second(self.a)))

        def s3(self):
            self.hop(self.span(self.b * 4, 4), self.at_b(first(self.b)))

        def s4(self):
            near = self.span(8 * (self.b // 2), 8)
            self.hop(near, self.at_b(second(self.b)))
            self.share = [
                remote(self.view(0, pl.ds(1, 3), near), self.view(1, pl.ds(1, 3), near), sibling)
            ]

        def s5(self):
            for copy in self.arrive:
                copy.wait_recv()
            rest = self.span(8 - 8 * (self.b // 2), 8)
            self.share.append(
                remote(self.view(0, pl.ds(1, 3), rest), self.view(1, pl.ds(1, 3), rest), sibling)
            )

        def s6(self):
            for copy in self.share:
                copy.wait_recv()

    class Group:
        def __init__(self, halves, own, own_src):
            self.halves = halves
            self.own, self.own_src = own, own_src

        def z(self):
            for half in self.halves:
                half.z()
            self.own_copies = [
                remote(src, dst.at[pl.ds(1, 1), pl.ds(0, 1)], sibling)
                for src, dst in zip(self.own_src, self.own)
            ]

        def run(self, stage):
            if stage == 0:
                return self.z()
            for half in self.halves:
                getattr(half, "s%d" % stage)()
            if stage == 6:
                for copy in self.own_copies:
                    copy.wait_recv()

    def four(ref, rows, columns):
        return ref.reshape(1, 1, rows, columns)

    def half_kv(kind, ref, buf):
        return Half(
            kind,
            lambda step, rows: four(ref, D, 128).at[0, :, rows, :],
            lambda e, d, rows: buf.at[e, d, rows, :],
            0, 64,
        )

    def half_up(kind, j):
        return Half(
            kind,
            lambda step, rows: four(up, D, 512).at[0, :, rows, pl.ds(j * 256, 256)],
            lambda e, d, rows: up_b.at[j, e, d, rows, :],
            kind * 512, 32,
        )

    def half_dn(kind, r):
        return Half(
            kind,
            lambda step, rows: four(dn, 512, D).at[0, :, rows, q_cols(r + step + 4)],
            lambda e, d, rows: dn_b.at[r, e, d, rows, :],
            kind * 256, 16,
        )

    groups = {
        "kv": Group([half_kv(0, wk, wk_b), half_kv(1, wv, wv_b)], [wk_b, wv_b],
                    [four(wk, D, 128), four(wv, D, 128)]),
    }
    for j in range(2):
        groups["u%d" % j] = Group(
            [half_up(0, j), half_up(1, j)], [up_b.at[j]],
            [four(up, D, 512).at[:, :, :, pl.ds(j * 256, 256)]],
        )
    for r in range(4):
        groups["d%d" % r] = Group(
            [half_dn(0, r), half_dn(1, r)], [dn_b.at[r]],
            [four(dn, 512, D).at[:, :, :, q_cols(r)]],
        )

    class Ring:
        def __init__(self, ref, buf, rows):
            self.ref, self.buf, self.rows = ref, buf, rows

        def run(self, stage):
            buf, half = self.buf, self.rows // 2
            if stage == 0:
                self.up = remote(self.ref, buf.at[0, 3], z_dev(1))
                self.down = remote(self.ref, buf.at[0, 1], z_dev(-1))
                self.share = [remote(self.ref, buf.at[1, 0], sibling)]
            elif stage == 1:
                self.up.wait_recv()
                self.down.wait_recv()
                high, low = pl.ds(half, half), pl.ds(0, half)
                self.far = [
                    remote(buf.at[0, 3, high], buf.at[0, 2, high], z_dev(1)),
                    remote(buf.at[0, 1, low], buf.at[0, 2, low], z_dev(-1)),
                ]
                self.share.append(remote(buf.at[0, 1], buf.at[1, 1], sibling))
                self.share.append(remote(buf.at[0, 3], buf.at[1, 3], sibling))
            elif stage == 2:
                for copy in self.far:
                    copy.wait_recv()
                self.share.append(remote(buf.at[0, 2], buf.at[1, 2], sibling))
            else:
                for copy in self.share:
                    copy.wait_recv()

    groups["wq"] = Ring(wq, wq_b, D)
    groups["wo"] = Ring(wo, wo_b, 128)

    plan = {
        "wq": (0.1, 6.0, 9.0, 11.0),
        "kv": (0.0, 1.5, 3.0, 5.0, 8.0, 13.0, 15.0),
        "u0": (0.3, 3.2, 5.2, 9.0, 13.1, 18.0, 20.0),
        "wo": (6.1, 12.0, 15.1, 17.0),
        "u1": (4.0, 9.1, 11.0, 14.0, 18.1, 25.0, 27.0),
        "d2": (8.0, 14.1, 16.0, 18.2, 25.1, 29.0, 30.5),
        "d1": (12.0, 18.3, 20.0, 25.2, 29.1, 33.0, 34.5),
        "d3": (16.0, 22.0, 24.0, 29.2, 33.1, 37.0, 38.5),
        "d0": (20.0, 26.0, 28.0, 33.2, 37.1, 41.0, 42.5),
    }
    order = list(plan)
    for name in order:
        for stage, when in enumerate(plan[name]):
            events.append((when, order.index(name), name, stage))
    events.sort()

    def pump(until):
        while events and events[0][0] <= until:
            _, _, name, stage = events.pop(0)
            groups[name].run(stage)

    def need(name, stage):
        while any(e[2] == name and e[3] <= stage for e in events):
            _, _, other, step = events.pop(0)
            groups[other].run(step)

    pump(0.2)
    halo_i = used[0]
    used[0] += 1
    halo = pltpu.make_async_remote_copy(
        src_ref=frames.at[rec, pl.ds(0, LOOK), :], dst_ref=xs.at[pl.ds(OWN, LOOK)],
        send_sem=send_sem.at[halo_i], recv_sem=recv_sem.at[halo_i],
        device_id=((tm + 31) % 32, mp), device_id_type=MESH,
    )

    @pl.when(c == 1)
    def _():
        halo.start()

    pump(0.3)
    first_row = tm * 640 + c * OWN
    live_end = valid[rec] - first_row

    xs_copy.wait()

    def norm_rows(i, carry):
        rows = pl.ds(pl.multiple_of(i * 32, 32), 32)
        nrm[rows, :] = normalize(xs[rows, :].astype(F32), g1[...]).astype(BF16)
        return carry

    lax.fori_loop(0, 5, norm_rows, 0)
    pump(1.5)
    lax.fori_loop(5, 10, norm_rows, 0)
    pump(3.2)

    @pl.when(c == 0)
    def _():
        pltpu.make_async_copy(
            frames.at[rec, pl.ds(OWN, LOOK), :], xs.at[pl.ds(OWN, LOOK)], loc_sem.at[look_sem]
        ).wait()

    @pl.when(c == 1)
    def _():
        halo.wait()

    norm_rows(10, 0)
    row_i = lax.broadcasted_iota(jnp.int32, (16, OWN), 0)
    col_i = lax.broadcasted_iota(jnp.int32, (16, OWN), 1)
    inside = (col_i >= row_i * SEG) & (col_i < row_i * SEG + SEG) & (col_i < live_end)
    picks = jnp.where(inside, 1.0, 0.0)
    counts = jnp.sum(picks, -1, keepdims=True)
    nrm[ROWS:EXT, :] = (
        dot(picks.astype(BF16), nrm[:OWN, :]) / jnp.maximum(counts, 1.0)
    ).astype(BF16)
    pump(11.0)
    for copy in own_copies:
        copy.wait()

    def project(buf, dest, scale):
        def step(p, carry):
            e, d = p // 2, 2 * (p % 2)
            weight = jnp.concatenate([buf[e, d], buf[e, d + 1]], axis=1)
            value = dot(nrm[...], weight).astype(BF16) * scale
            dest[2 * p] = value[:, :128]
            dest[2 * p + 1] = value[:, 128:]
            return carry

        lax.fori_loop(0, 4, step, 0)

    need("wq", 3)
    project(wq_b, qb, jnp.asarray(0.125, BF16))
    need("kv", 6)
    project(wk_b, kb, jnp.asarray(1.0, BF16))
    project(wv_b, vb, jnp.asarray(1.0, BF16))
    pump(18.0)

    head_r = lax.broadcasted_iota(jnp.int32, (32, 128), 0) % 16
    head_l = lax.broadcasted_iota(jnp.int32, (32, 128), 1) // 64
    scores = jnp.zeros((32, ROWS), F32)
    for t in range(8):
        asked = qb[t, ROWS:EXT, :].astype(F32)
        rows = jnp.concatenate(
            [jnp.broadcast_to(asked[s : s + 1], (16, 128)) for s in range(2)], axis=0
        )
        rows = jnp.where(head_r == head_l + 2 * t, rows, 0.0).astype(BF16)
        scores = scores + dot_t(rows, kb[t, :ROWS, :])
    seg_r = lax.broadcasted_iota(jnp.int32, (32, ROWS), 0) // 16
    key_l = lax.broadcasted_iota(jnp.int32, (32, ROWS), 1)
    ok = (key_l >= seg_r * SEG) & (key_l < seg_r * SEG + KEYS) & (key_l < live_end)
    scores = jnp.where(ok, scores, NEG)
    p = jnp.exp(scores - jnp.max(scores, -1, keepdims=True))
    p = (p / jnp.sum(p, -1, keepdims=True)).astype(BF16)
    parts = []
    for t in range(8):
        got = dot(p, vb[t, :ROWS, :])
        got = jnp.where(head_r == head_l + 2 * t, got, 0.0)
        parts.append(
            jnp.concatenate(
                [jnp.sum(got[s * 16 : s * 16 + 16], 0, keepdims=True) for s in range(2)], axis=0
            )
        )
    summed = jnp.concatenate(parts, axis=1)
    summed = jnp.concatenate([summed, jnp.zeros((14, D), F32)], axis=0).astype(BF16)
    need("wo", 3)
    memory = dot(summed, wo_b[...].reshape(D, D)).astype(BF16).astype(F32)
    for s in range(2):
        for b in range(8):
            mrow[s * 8 + b : s * 8 + b + 1, :] = memory[s : s + 1, b * 128 : b * 128 + 128]
    mine = pl.ds(pl.multiple_of(c * 16, 16), 16)
    mem_b[tm, mine, :] = mrow[...].astype(BF16)
    pair = remote(mem_b.at[tm, mine], mem_b.at[tm, mine], sibling)
    pump(20.0)
    pair.wait_recv()

    base = used[0]
    used[0] += 31

    def bank_copy(i):
        return pltpu.make_async_remote_copy(
            src_ref=mem_b.at[tm], dst_ref=mem_b.at[tm],
            send_sem=send_sem.at[base + i], recv_sem=recv_sem.at[base + i],
            device_id=((tm + 1 + i) % 32, mp), device_id_type=MESH,
        )

    def bank_send(i, carry):
        bank_copy(i).start()
        return carry

    lax.fori_loop(0, 31, bank_send, 0)
    pump(25.2)

    def bank_wait(i, carry):
        bank_copy(i).wait()
        return carry

    lax.fori_loop(0, 31, bank_wait, 0)

    memf[...] = mem_b[...].reshape(SLOTS * 8, 128).astype(F32)
    mem = jnp.concatenate(
        [memf[pl.ds(b, SLOTS, stride=8), :] for b in range(8)], axis=1
    ).astype(BF16)

    def bank_project(buf, dest):
        def step(p, carry):
            e, d = p // 2, 2 * (p % 2)
            weight = jnp.concatenate([buf[e, d], buf[e, d + 1]], axis=1)
            value = dot(mem, weight).astype(BF16)
            dest[2 * p] = value[:, :128]
            dest[2 * p + 1] = value[:, 128:]
            return carry

        lax.fori_loop(0, 4, step, 0)

    bank_project(wk_b, bk)
    bank_project(wv_b, bv)
    pump(28.0)

    lane = lax.broadcasted_iota(jnp.int32, (SEG, 128), 1)
    near_l = lax.broadcasted_iota(jnp.int32, (2 * SEG, KEYS), 1)
    far_l = lax.broadcasted_iota(jnp.int32, (2 * SEG, SLOTS), 1)
    for s in range(2):
        near_ok = near_l < live_end - s * SEG
        far_ok = (far_l < tm * 4 + c * 2 + s) & (far_l * SEG < live_end + first_row)
        rows, keys = slice(s * SEG, s * SEG + SEG), slice(s * SEG, s * SEG + KEYS)

        def heads(t, carry, rows=rows, keys=keys, near_ok=near_ok, far_ok=far_ok):
            q = qb[t, rows, :]
            zero = jnp.zeros_like(q)
            q = jnp.concatenate([jnp.where(lane < 64, q, zero), jnp.where(lane < 64, zero, q)], 0)
            near = jnp.where(near_ok, dot_t(q, kb[t, keys, :]), NEG)
            far = jnp.where(far_ok, dot_t(q, bk[t]), NEG)
            top = jnp.maximum(jnp.max(near, -1, keepdims=True), jnp.max(far, -1, keepdims=True))
            near = jnp.exp(near - top)
            far = jnp.exp(far - top)
            total = jnp.sum(near, -1, keepdims=True) + jnp.sum(far, -1, keepdims=True)
            got = dot(near.astype(BF16), vb[t, keys, :]) + dot(far.astype(BF16), bv[t])
            got = got / total
            got = jnp.where(lane < 64, got[:SEG], got[SEG:]).astype(BF16)
            fo[rows, pl.ds(pl.multiple_of(t * 128, 128), 128)] = got
            return carry

        lax.fori_loop(0, 4, heads, 0)
        pump(29.0 + 4 * s)
        lax.fori_loop(4, 8, heads, 0)
        pump(30.5 + 4 * s)

    for n in range(4):
        weight = wo_b[:, :, :, n * 256 : n * 256 + 256].reshape(D, 256)
        mixed[n] = dot(fo[...], weight) + xs[:OWN, n * 256 : n * 256 + 256].astype(F32)
    pump(36.0)

    def norm_two(i, carry):
        rows = pl.ds(pl.multiple_of(i * 32, 32), 32)
        v = jnp.concatenate([mixed[n, rows, :] for n in range(4)], axis=1)
        n2[rows, :] = normalize(v, g2[...]).astype(BF16)
        return carry

    lax.fori_loop(0, 10, norm_two, 0)

    for j in range(2):
        need("u%d" % j, 6)

        def up_step(b, carry, j=j):
            h = dot(n2[...], up_b[j, b // 4, b % 4])
            h = 0.5 * h * (1.0 + lax.erf(h * (2.0 ** -0.5)))
            hid[:, pl.ds(pl.multiple_of(b * 512 + j * 256, 256), 256)] = h.astype(BF16)
            return carry

        for k in range(4):
            lax.fori_loop(2 * k, 2 * k + 2, up_step, 0)
            pump(36.0 + 4 * j + k)

    outs = []
    row_span = pl.ds(pl.multiple_of(c * OWN, OWN), OWN)
    for r in (2, 1, 3, 0):
        need("d%d" % r, 6)
        block = dot(hid[...], dn_b[r].reshape(4 * D, 256))
        to = (zl + r) % 4
        block = (block + mixed[to]).astype(BF16)
        ob[r, 0] = block[:, :128]
        ob[r, 1] = block[:, 128:]
        if r:
            for e in range(2):
                core = c if e == 0 else 1 - c
                outs.append(remote(ob.at[r, core], out.at[rec, row_span, :], (tm, to * 2 + core)))
        else:
            outs.append(remote(ob.at[0, 1 - c], out.at[rec, row_span, :], sibling))
            home = local(ob.at[0, c], out.at[rec, row_span, :])
    home.wait()
    for copy in outs:
        copy.wait_recv()
    for copy in sent:
        copy.wait_send()
    assert used[0] <= N_SEM, used[0]


def body(frames, valid, ln1_gain, w_query, w_key, w_value, w_out, ln2_gain, w_up, w_down):
    vmem = pl.BlockSpec(memory_space=pltpu.VMEM)
    anywhere = pl.BlockSpec(memory_space=pl.ANY)
    scratch = [
        pltpu.VMEM((ROWS, D), BF16),
        pltpu.VMEM((EXT, D), BF16),
        pltpu.VMEM((8, EXT, 128), BF16),
        pltpu.VMEM((8, EXT, 128), BF16),
        pltpu.VMEM((8, EXT, 128), BF16),
        pltpu.VMEM((2, 4, D, 128), BF16),
        pltpu.VMEM((2, 4, D, 128), BF16),
        pltpu.VMEM((2, 4, D, 128), BF16),
        pltpu.VMEM((2, 4, 128, D), BF16),
        pltpu.VMEM((2, 2, 4, D, 256), BF16),
        pltpu.VMEM((4, 2, 4, 512, 256), BF16),
        pltpu.VMEM((16, 128), F32),
        pltpu.VMEM((32, 32, 128), BF16),
        pltpu.VMEM((SLOTS * 8, 128), F32),
        pltpu.VMEM((8, SLOTS, 128), BF16),
        pltpu.VMEM((8, SLOTS, 128), BF16),
        pltpu.VMEM((OWN, D), BF16),
        pltpu.VMEM((4, OWN, 256), F32),
        pltpu.VMEM((OWN, D), BF16),
        pltpu.VMEM((OWN, 4 * D), BF16),
        pltpu.VMEM((4, 2, OWN, 128), BF16),
        pltpu.SemaphoreType.DMA((16,)),
        pltpu.SemaphoreType.DMA((N_SEM,)),
        pltpu.SemaphoreType.DMA((N_SEM,)),
    ]
    return pl.pallas_call(
        kernel,
        name="layer",
        out_shape=jax.ShapeDtypeStruct((frames.shape[0], frames.shape[1], 128), BF16),
        in_specs=[pl.BlockSpec(memory_space=pltpu.SMEM), vmem, vmem] + [anywhere] * 7,
        out_specs=anywhere,
        scratch_shapes=scratch,
        compiler_params=pltpu.CompilerParams(
            collective_id=0, has_side_effects=True, vmem_limit_bytes=56 * 2**20
        ),
    )(
        valid, ln1_gain.reshape(1, D), ln2_gain.reshape(1, D),
        frames, w_query, w_key, w_value, w_out, w_up, w_down,
    )


def solution(mesh):
    placed = (
        P(None, "tm", None),
        P(),
        P(),
        P(None, "mp"),
        P(None, "mp"),
        P(None, "mp"),
        P("mp", None),
        P(),
        P(None, "mp"),
        P("mp", None),
    )
    return jax.shard_map(
        body, mesh=mesh, in_specs=placed, out_specs=P(None, "tm", "mp"), check_vma=False
    )
```

```python
import jax
import jax.numpy as jnp
from jax import lax
from jax.experimental import pallas as pl
from jax.experimental.pallas import tpu as pltpu
from jax.sharding import PartitionSpec as P

MESH = pl.DeviceIdType.MESH
F32 = jnp.float32
BF16 = jnp.bfloat16

D = 1024
SEG = 160
LOOK = 32
KEYS = SEG + LOOK
OWN = 2 * SEG
ROWS = OWN + LOOK
EXT = ROWS + 16
SLOTS = 128
EPS = 1e-05
NEG = -1e30
N_SEM = 232

SCHEDULE = (
    "norm_one enter k:0 v:0",
    "wq:0 look k:1 v:1",
    "u0:0 k:2 meet sums",
    "v:2 wq:1 wo:0 k:3",
    "u1:0 v:3 u0:1 d2:0",
    "wq:2 k:4 k0 v:4",
    "d1:0 k:5 k1 d3:0",
    "wo:1 u0:2 v0 v:5",
    "v1 d0:0 u1:1 d2:1",
    "d1:1 d3:1 wo:2 q0",
    "u0:3 wq:3 q1 summary",
    "u1:2 d0:1 wo:3 memory",
    "d2:2 near0 d1:2 bank_a",
    "d3:2 near1 near2 near3",
    "u0:4 u1:3 bank_b d0:2",
    "d2:3 d1:3 d3:3 bank_c",
    "bank_d far0 u1:4 far1",
    "far2 d0:3 far3 d2:4",
    "mix norm_two d1:4 up00",
    "up01 u0:5 up02 d3:4",
    "up03 up10 d0:4 up11",
    "u1:5 up12 up13 d2:5",
    "down2 d1:5 down1 d3:5",
    "down3 d0:5 down0",
)


def dot(a, b):
    return jnp.dot(a, b, preferred_element_type=F32)


def normalize(x, gain):
    mean = jnp.sum(x, -1, keepdims=True) * (1.0 / D)
    square = jnp.sum(x * x, -1, keepdims=True) * (1.0 / D)
    return (x - mean) * lax.rsqrt(square - mean * mean + EPS) * gain


def kernel(
    valid, g1, g2, frames, wq, wk, wv, wo, up, dn, out,
    xs, nrm, qb, kt, vb, wq_b, wk_b, wv_b, wo_b, up_b, dn_b,
    mrow, mem_b, memf, bk, bv, acc, mx, fo, mixed, n2, hid, ob,
    loc_sem, send_sem, recv_sem, hello,
):
    tm = lax.axis_index("tm")
    mp = lax.axis_index("mp")
    x = tm // 8
    y = (tm // 2) % 4
    zl = mp // 2
    z = (tm % 2) * 4 + zl
    c = mp % 2
    rec = zl

    def dev(px, py, pz, pc):
        return ((px * 4 + py) * 2 + pz // 4, (pz % 4) * 2 + pc)

    def z_dev(step):
        return dev(x, y, (z + step + 8) % 8, c)

    sibling = (tm, zl * 2 + 1 - c)

    barrier = pltpu.get_barrier_semaphore()

    across = ((zl + 2) % 4) * 2 + c
    before, after = ((tm + 31) % 32, across), ((tm + 1) % 32, across)
    greeted = [before, after] + [z_dev(step) for step in (1, -1, 2, -2)]
    greeted += [(tm, (mp + i) % 8) for i in range(1, 8)]
    along = [dev((x + i) % 4, y, z, c) for i in (2, 1, 3)]
    bank_one = [dev((x + i) % 4, y, (z + 4) % 8, c) for i in (2, 1, 3, 0)] + along
    bank_two = [dev(x, (y + i) % 4, z, c) for i in (2, 1, 3)]
    greeted += along + bank_two
    for other in greeted:
        pl.semaphore_signal(barrier, inc=1, device_id=other, device_id_type=MESH)

    used = [0]
    sent = []

    def remote(src, dst, to):
        i = used[0]
        used[0] += 1
        copy = pltpu.make_async_remote_copy(
            src_ref=src, dst_ref=dst, send_sem=send_sem.at[i], recv_sem=recv_sem.at[i],
            device_id=to, device_id_type=MESH,
        )
        sent.append(copy)
        copy.start()
        return copy

    n_local = [0]

    def local(src, dst):
        i = n_local[0]
        n_local[0] += 1
        copy = pltpu.make_async_copy(src, dst, loc_sem.at[i])
        copy.start()
        return copy

    xs_copy = local(frames.at[rec, pl.ds(c * OWN, OWN), :], xs.at[pl.ds(0, OWN)])
    own_copies = [
        local(wq, wq_b.at[0, 0]), local(wk, wk_b.at[0, 0]), local(wv, wv_b.at[0, 0]),
        local(wo, wo_b.at[0, 0]),
    ]
    for j in range(2):
        own_copies.append(local(up.at[:, pl.ds(j * 256, 256)], up_b.at[j, 0, 0]))

    def q_cols(step):
        return pl.ds(pl.multiple_of(((zl + step) % 4) * 256, 256), 256)

    for r in range(4):
        own_copies.append(local(dn.at[:, q_cols(r)], dn_b.at[r, 0, 0]))

    look_sem = n_local[0]
    n_local[0] += 1

    @pl.when(c == 0)
    def _():
        pltpu.make_async_copy(
            frames.at[rec, pl.ds(OWN, LOOK), :], xs.at[pl.ds(OWN, LOOK)], loc_sem.at[look_sem]
        ).start()

    lx = (x + c) % 4
    ly = (y + c) % 4

    def at_x(label):
        return dev((label + 4 - c) % 4, y, z, c)

    def at_y(label):
        return dev(x, (label + 4 - c) % 4, z, c)

    def first(label):
        return label + 1 - 2 * (label % 2)

    def second(label):
        return 3 - label

    class Half:
        def __init__(self, kind, source, view, base, rows):
            self.source, self.view, self.base, self.rows = source, view, base, rows
            if kind == 0:
                self.a, self.b, self.at_a, self.at_b = lx, ly, at_x, at_y
            else:
                self.a, self.b, self.at_a, self.at_b = ly, lx, at_y, at_x
            self.far = 2 if kind == 0 else -2

        def span(self, index, count):
            return pl.ds(pl.multiple_of(self.base + index * self.rows, self.rows), count * self.rows)

        def z(self):
            here = self.span(self.b * 4 + self.a, 1)
            self.arrive = [
                remote(self.source(1, here), self.view(0, pl.ds(3, 1), here), z_dev(1)),
                remote(self.source(-1, here), self.view(0, pl.ds(1, 1), here), z_dev(-1)),
                remote(self.source(self.far, here), self.view(0, pl.ds(2, 1), here), z_dev(self.far)),
            ]

        def hop(self, rows, to):
            for copy in self.arrive:
                copy.wait_recv()
            part = self.view(0, pl.ds(1, 3), rows)
            self.arrive = [remote(part, part, to)]

        def s1(self):
            for copy in self.arrive:
                copy.wait_recv()
            part = self.view(0, pl.ds(1, 3), self.span(self.b * 4 + self.a, 1))
            self.arrive = [remote(part, part, self.at_a((self.a + i) % 4)) for i in (2, 1, 3)]

        def s2(self):
            self.hop(self.span(self.b * 4, 4), self.at_b(first(self.b)))

        def s3(self):
            near = self.span(8 * (self.b // 2), 8)
            self.hop(near, self.at_b(second(self.b)))
            self.share = [
                remote(self.view(0, pl.ds(1, 3), near), self.view(1, pl.ds(1, 3), near), sibling)
            ]

        def s4(self):
            for copy in self.arrive:
                copy.wait_recv()
            rest = self.span(8 - 8 * (self.b // 2), 8)
            self.share.append(
                remote(self.view(0, pl.ds(1, 3), rest), self.view(1, pl.ds(1, 3), rest), sibling)
            )

        def s5(self):
            for copy in self.share:
                copy.wait_recv()

    class Group:
        def __init__(self, halves, own, own_src):
            self.halves = halves
            self.own, self.own_src = own, own_src

        def z(self):
            for half in self.halves:
                half.z()
            self.own_copies = [
                remote(src, dst.at[pl.ds(1, 1), pl.ds(0, 1)], sibling)
                for src, dst in zip(self.own_src, self.own)
            ]

        def run(self, stage):
            if stage == 0:
                return self.z()
            for half in self.halves:
                getattr(half, "s%d" % stage)()
            if stage == 5:
                for copy in self.own_copies:
                    copy.wait_recv()

    def four(ref, rows, columns):
        return ref.reshape(1, 1, rows, columns)

    def half_kv(kind, ref, buf):
        return Half(
            kind,
            lambda step, rows: four(ref, D, 128).at[0, :, rows, :],
            lambda e, d, rows: buf.at[e, d, rows, :],
            kind * 512, 32,
        )

    def half_up(kind, j):
        return Half(
            kind,
            lambda step, rows: four(up, D, 512).at[0, :, rows, pl.ds(j * 256, 256)],
            lambda e, d, rows: up_b.at[j, e, d, rows, :],
            kind * 512, 32,
        )

    def half_dn(kind, r):
        return Half(
            kind,
            lambda step, rows: four(dn, 512, D).at[0, :, rows, q_cols(r + step + 4)],
            lambda e, d, rows: dn_b.at[r, e, d, rows, :],
            kind * 256, 16,
        )

    groups = {
        "k": Group([half_kv(0, wk, wk_b), half_kv(1, wk, wk_b)], [wk_b], [four(wk, D, 128)]),
        "v": Group([half_kv(0, wv, wv_b), half_kv(1, wv, wv_b)], [wv_b], [four(wv, D, 128)]),
    }
    for j in range(2):
        groups["u%d" % j] = Group(
            [half_up(0, j), half_up(1, j)], [up_b.at[j]],
            [four(up, D, 512).at[:, :, :, pl.ds(j * 256, 256)]],
        )
    for r in range(4):
        groups["d%d" % r] = Group(
            [half_dn(0, r), half_dn(1, r)], [dn_b.at[r]],
            [four(dn, 512, D).at[:, :, :, q_cols(r)]],
        )

    class Ring:
        def __init__(self, ref, buf, rows):
            self.ref, self.buf, self.rows = ref, buf, rows

        def run(self, stage):
            buf, half = self.buf, self.rows // 2
            if stage == 0:
                self.up = remote(self.ref, buf.at[0, 3], z_dev(1))
                self.down = remote(self.ref, buf.at[0, 1], z_dev(-1))
                self.share = [remote(self.ref, buf.at[1, 0], sibling)]
            elif stage == 1:
                self.up.wait_recv()
                self.down.wait_recv()
                high, low = pl.ds(half, half), pl.ds(0, half)
                self.far = [
                    remote(buf.at[0, 3, high], buf.at[0, 2, high], z_dev(1)),
                    remote(buf.at[0, 1, low], buf.at[0, 2, low], z_dev(-1)),
                ]
                self.share.append(remote(buf.at[0, 1], buf.at[1, 1], sibling))
                self.share.append(remote(buf.at[0, 3], buf.at[1, 3], sibling))
            elif stage == 2:
                for copy in self.far:
                    copy.wait_recv()
                self.share.append(remote(buf.at[0, 2], buf.at[1, 2], sibling))
            else:
                for copy in self.share:
                    copy.wait_recv()

    groups["wq"] = Ring(wq, wq_b, D)
    groups["wo"] = Ring(wo, wo_b, 128)

    halo_i = used[0]
    used[0] += 1
    halo = pltpu.make_async_remote_copy(
        src_ref=frames.at[(zl + 2) % 4, pl.ds(0, LOOK), :], dst_ref=xs.at[pl.ds(OWN, LOOK)],
        send_sem=send_sem.at[halo_i], recv_sem=recv_sem.at[halo_i],
        device_id=before, device_id_type=MESH,
    )
    first_row = tm * 640 + c * OWN
    live_end = valid[rec] - first_row
    acts = {}

    def action(f):
        acts[f.__name__] = f
        return f

    def loop(f, lo, hi, unroll=1):
        lax.fori_loop(lo, hi, lambda i, carry: (f(i), carry)[1], 0, unroll=unroll)

    @action
    def enter():
        pl.semaphore_wait(barrier, len(greeted))

    @action
    def look():
        pl.semaphore_signal(hello.at[0], inc=1, device_id=z_dev(-2), device_id_type=MESH)

        @pl.when(c == 1)
        def _():
            halo.start()

    @action
    def meet():
        pl.semaphore_wait(hello.at[0], 1)
        for other in along:
            pl.semaphore_signal(hello.at[1], inc=1, device_id=other, device_id_type=MESH)

    def norm_rows(i):
        rows = pl.ds(pl.multiple_of(i * 32, 32), 32)
        nrm[rows, :] = normalize(xs[rows, :].astype(F32), g1[...]).astype(BF16)

    @action
    def norm_one():
        xs_copy.wait()
        loop(norm_rows, 0, 10, unroll=2)

    @action
    def sums():
        @pl.when(c == 0)
        def _():
            pltpu.make_async_copy(
                frames.at[rec, pl.ds(OWN, LOOK), :], xs.at[pl.ds(OWN, LOOK)], loc_sem.at[look_sem]
            ).wait()

        @pl.when(c == 1)
        def _():
            halo.wait()

        norm_rows(10)
        row_i = lax.broadcasted_iota(jnp.int32, (16, OWN), 0)
        col_i = lax.broadcasted_iota(jnp.int32, (16, OWN), 1)
        inside = (col_i >= row_i * SEG) & (col_i < row_i * SEG + SEG) & (col_i < live_end)
        picks = jnp.where(inside, 1.0, 0.0)
        counts = jnp.sum(picks, -1, keepdims=True)
        nrm[ROWS:EXT, :] = (
            dot(picks.astype(BF16), nrm[:OWN, :]) / jnp.maximum(counts, 1.0)
        ).astype(BF16)
        for copy in own_copies:
            copy.wait()

    def project(left, buf, dest, p, scale=None):
        e, d = p // 2, 2 * (p % 2)
        weight = jnp.concatenate([buf[e, d], buf[e, d + 1]], axis=1)
        value = dot(left, weight).astype(BF16)
        if scale is not None:
            value = value * jnp.asarray(scale, BF16)
        dest[2 * p] = value[:, :128]
        dest[2 * p + 1] = value[:, 128:]

    def project_keys(p):
        e, d = p // 2, 2 * (p % 2)
        weight = jnp.concatenate([wk_b[e, d], wk_b[e, d + 1]], axis=1)
        value = dot(nrm[:ROWS, :], weight)
        for s in range(2):
            turned = value[s * SEG : s * SEG + KEYS].T.astype(BF16)
            kt[s, 2 * p] = turned[:128]
            kt[s, 2 * p + 1] = turned[128:]

    for e in range(2):
        span = (2 * e, 2 * e + 2)
        acts["q%d" % e] = lambda span=span: loop(
            lambda p: project(nrm[...], wq_b, qb, p, 0.125), *span)
        acts["k%d" % e] = lambda span=span: loop(project_keys, *span)
        acts["v%d" % e] = lambda span=span: loop(lambda p: project(nrm[...], wv_b, vb, p), *span)

    held = {}

    @action
    def summary():
        head_r = lax.broadcasted_iota(jnp.int32, (16, 128), 0)
        head_l = lax.broadcasted_iota(jnp.int32, (16, 128), 1) // 64
        key_l = lax.broadcasted_iota(jnp.int32, (16, KEYS), 1)
        parts = []
        for s in range(2):
            parts.append(jnp.zeros((16, KEYS), F32))
            for t in range(8):
                asked = qb[t, ROWS:EXT, :].astype(F32)
                rows = jnp.broadcast_to(asked[s : s + 1], (16, 128))
                rows = jnp.where(head_r == head_l + 2 * t, rows, 0.0).astype(BF16)
                parts[s] = parts[s] + dot(rows, kt[s, t])
            parts[s] = jnp.where(key_l < live_end - s * SEG, parts[s], NEG)
        scores = jnp.concatenate(parts, axis=0)
        p = jnp.exp(scores - jnp.max(scores, -1, keepdims=True))
        p = (p / jnp.sum(p, -1, keepdims=True)).astype(BF16)
        parts = []
        for t in range(8):
            rows = []
            for s in range(2):
                got = dot(p[s * 16 : s * 16 + 16], vb[t, s * SEG : s * SEG + KEYS, :])
                got = jnp.where(head_r == head_l + 2 * t, got, 0.0)
                rows.append(jnp.sum(got, 0, keepdims=True))
            parts.append(jnp.concatenate(rows, axis=0))
        summed = jnp.concatenate(parts, axis=1)
        held["summed"] = jnp.concatenate([summed, jnp.zeros((14, D), F32)], axis=0).astype(BF16)

    mine = pl.ds(pl.multiple_of(c * 16, 16), 16)
    zh = tm % 2

    @action
    def memory():
        got = dot(held["summed"], wo_b[...].reshape(D, D)).astype(BF16).astype(F32)
        for s in range(2):
            for b in range(8):
                mrow[s * 8 + b : s * 8 + b + 1, :] = got[s : s + 1, b * 128 : b * 128 + 128]
        mem_b[x, y, zh, mine, :] = mrow[...].astype(BF16)
        part = mem_b.at[x, y, zh, mine]
        held["pair"] = remote(part, part, sibling)

    @action
    def bank_a():
        pl.semaphore_wait(hello.at[1], 3)
        held["pair"].wait_recv()
        part = mem_b.at[x, y, zh]
        held["bank"] = [remote(part, part, other) for other in bank_one]

    @action
    def bank_b():
        for copy in held["bank"]:
            copy.wait_recv()
        part = mem_b.at[:, pl.ds(y, 1)]
        held["bank"] = [remote(part, part, other) for other in bank_two]

    @action
    def bank_c():
        for copy in held["bank"]:
            copy.wait_recv()
        memf[...] = mem_b[...].reshape(SLOTS * 8, 128).astype(F32)
        mem = jnp.concatenate(
            [memf[pl.ds(b, SLOTS, stride=8), :] for b in range(8)], axis=1
        ).astype(BF16)
        held["mem"] = mem

        def keys(p):
            e, d = p // 2, 2 * (p % 2)
            weight = jnp.concatenate([wk_b[e, d], wk_b[e, d + 1]], axis=1)
            turned = dot(mem, weight).T.astype(BF16)
            bk[2 * p] = turned[:128]
            bk[2 * p + 1] = turned[128:]

        loop(keys, 0, 4)

    @action
    def bank_d():
        mem = held["mem"]
        loop(lambda p: project(mem, wv_b, bv, p), 0, 4)

    lane = lax.broadcasted_iota(jnp.int32, (SEG, 128), 1)

    def one_head(s, t, h):
        q = qb[t, s * SEG : s * SEG + SEG, :]
        mine = lane < 64 if h == 0 else lane >= 64
        return jnp.where(mine, q, jnp.zeros_like(q))

    def with_ones(v):
        return jnp.concatenate([v, jnp.ones_like(v)], axis=1)

    def near_step(s, t):
        keys = slice(s * SEG, s * SEG + KEYS)
        near_l = lax.broadcasted_iota(jnp.int32, (SEG, KEYS), 1)
        ones = with_ones(vb[t, keys, :])
        for h in range(2):
            near = dot(one_head(s, t, h), kt[s, t])
            near = jnp.where(near_l < live_end - s * SEG, near, NEG)
            top = jnp.max(near, -1, keepdims=True)
            near = jnp.exp(near - top).astype(BF16)
            rows = slice(h * SEG, h * SEG + SEG)
            acc[s * 8 + t, rows] = dot(near, ones)
            mx[s * 8 + t, rows] = jnp.broadcast_to(top, (SEG, 128))

    def far_step(s, t):
        far_l = lax.broadcasted_iota(jnp.int32, (SEG, SLOTS), 1)
        far_ok = (far_l < tm * 4 + c * 2 + s) & (far_l * SEG < live_end + first_row)
        both = []
        for h in range(2):
            rows = slice(h * SEG, h * SEG + SEG)
            far = jnp.where(far_ok, dot(one_head(s, t, h), bk[t]), NEG)
            before = mx[s * 8 + t, rows]
            top = jnp.maximum(before, jnp.max(far, -1, keepdims=True))
            far = jnp.exp(far - top).astype(BF16)
            keep = jnp.exp(before - top)
            got = dot(far, with_ones(bv[t]))
            total = acc[s * 8 + t, rows, 128:] * keep + got[:, 128:]
            both.append((acc[s * 8 + t, rows, :128] * keep + got[:, :128]) / total)
        got = jnp.where(lane < 64, both[0], both[1]).astype(BF16)
        fo[s * SEG : s * SEG + SEG, pl.ds(pl.multiple_of(t * 128, 128), 128)] = got

    for s in range(2):
        for half in range(2):
            span = (4 * half, 4 * half + 4)
            acts["near%d" % (2 * s + half)] = lambda s=s, span=span: loop(
                lambda t: near_step(s, t), *span, unroll=2)
            acts["far%d" % (2 * s + half)] = lambda s=s, span=span: loop(
                lambda t: far_step(s, t), *span, unroll=2)

    @action
    def mix():
        for n in range(4):
            weight = wo_b[:, :, :, n * 256 : n * 256 + 256].reshape(D, 256)
            mixed[n] = dot(fo[...], weight) + xs[:OWN, n * 256 : n * 256 + 256].astype(F32)

    @action
    def norm_two():
        def step(i):
            rows = pl.ds(pl.multiple_of(i * 32, 32), 32)
            v = jnp.concatenate([mixed[n, rows, :] for n in range(4)], axis=1)
            n2[rows, :] = normalize(v, g2[...]).astype(BF16)

        loop(step, 0, 10, unroll=2)

    def up_step(j, b):
        h = dot(n2[...], up_b[j, b // 4, b % 4])
        h = 0.5 * h * (1.0 + lax.erf(h * (2.0 ** -0.5)))
        hid[:, pl.ds(pl.multiple_of(b * 512 + j * 256, 256), 256)] = h.astype(BF16)

    for j in range(2):
        for k in range(4):
            acts["up%d%d" % (j, k)] = lambda j=j, k=k: loop(
                lambda b: up_step(j, b), 2 * k, 2 * k + 2)

    outs = []
    row_span = pl.ds(pl.multiple_of(c * OWN, OWN), OWN)

    def down(r):
        block = dot(hid[...], dn_b[r].reshape(4 * D, 256))
        to = (zl + r) % 4
        block = (block + mixed[to]).astype(BF16)
        ob[r, 0] = block[:, :128]
        ob[r, 1] = block[:, 128:]
        if r:
            for core in (c, 1 - c):
                outs.append(remote(ob.at[r, core], out.at[rec, row_span, :], (tm, to * 2 + core)))
        else:
            outs.append(remote(ob.at[0, 1 - c], out.at[rec, row_span, :], sibling))
            held["home"] = local(ob.at[0, c], out.at[rec, row_span, :])

    for r in range(4):
        acts["down%d" % r] = lambda r=r: down(r)

    for token in " ".join(SCHEDULE).split():
        if ":" in token:
            name, stage = token.split(":")
            groups[name].run(int(stage))
        else:
            acts[token]()
    held["home"].wait()
    for copy in outs:
        copy.wait_recv()
    for copy in sent:
        copy.wait_send()
    assert used[0] <= N_SEM, used[0]


def body(frames, valid, ln1_gain, w_query, w_key, w_value, w_out, ln2_gain, w_up, w_down):
    vmem = pl.BlockSpec(memory_space=pltpu.VMEM)
    anywhere = pl.BlockSpec(memory_space=pl.ANY)
    scratch = [
        pltpu.VMEM((ROWS, D), BF16),
        pltpu.VMEM((EXT, D), BF16),
        pltpu.VMEM((8, EXT, 128), BF16),
        pltpu.VMEM((2, 8, 128, KEYS), BF16),
        pltpu.VMEM((8, EXT, 128), BF16),
        pltpu.VMEM((2, 4, D, 128), BF16),
        pltpu.VMEM((2, 4, D, 128), BF16),
        pltpu.VMEM((2, 4, D, 128), BF16),
        pltpu.VMEM((2, 4, 128, D), BF16),
        pltpu.VMEM((2, 2, 4, D, 256), BF16),
        pltpu.VMEM((4, 2, 4, 512, 256), BF16),
        pltpu.VMEM((16, 128), F32),
        pltpu.VMEM((4, 4, 2, 32, 128), BF16),
        pltpu.VMEM((SLOTS * 8, 128), F32),
        pltpu.VMEM((8, SLOTS, 128), BF16),
        pltpu.VMEM((8, SLOTS, 128), BF16),
        pltpu.VMEM((16, OWN, 256), F32),
        pltpu.VMEM((16, OWN, 128), F32),
        pltpu.VMEM((OWN, D), BF16),
        pltpu.VMEM((4, OWN, 256), F32),
        pltpu.VMEM((OWN, D), BF16),
        pltpu.VMEM((OWN, 4 * D), BF16),
        pltpu.VMEM((4, 2, OWN, 128), BF16),
        pltpu.SemaphoreType.DMA((16,)),
        pltpu.SemaphoreType.DMA((N_SEM,)),
        pltpu.SemaphoreType.DMA((N_SEM,)),
        pltpu.SemaphoreType.REGULAR((2,)),
    ]
    return pl.pallas_call(
        kernel,
        name="layer",
        out_shape=jax.ShapeDtypeStruct((frames.shape[0], frames.shape[1], 128), BF16),
        in_specs=[pl.BlockSpec(memory_space=pltpu.SMEM), vmem, vmem] + [anywhere] * 7,
        out_specs=anywhere,
        scratch_shapes=scratch,
        compiler_params=pltpu.CompilerParams(
            collective_id=0, has_side_effects=True, vmem_limit_bytes=56 * 2**20
        ),
    )(
        valid, ln1_gain.reshape(1, D), ln2_gain.reshape(1, D),
        frames, w_query, w_key, w_value, w_out, w_up, w_down,
    )


def solution(mesh):
    placed = (
        P(None, "tm", None),
        P(),
        P(),
        P(None, "mp"),
        P(None, "mp"),
        P(None, "mp"),
        P("mp", None),
        P(),
        P(None, "mp"),
        P("mp", None),
    )
    return jax.shard_map(
        body, mesh=mesh, in_specs=placed, out_specs=P(None, "tm", "mp"), check_vma=False
    )
```

```python
import jax
import jax.numpy as jnp
from jax import lax
from jax.experimental import pallas as pl
from jax.experimental.pallas import tpu as pltpu
from jax.sharding import PartitionSpec as P

MESH = pl.DeviceIdType.MESH
F32 = jnp.float32
BF16 = jnp.bfloat16

D = 1024
SEG = 160
LOOK = 32
KEYS = SEG + LOOK
OWN = 2 * SEG
SPAN = 4 * SEG
SLOTS = 128
EPS = 1e-05
NEG = -1e30
N_SEM = 192

SCHEDULE = (
    "pre0 pre2 pre4 pre6",
    "enter u0:0 wo:0 u1:0",
    "look pre1 pre3 pre5",
    "d2:0 pre7 u0:1 d1:0",
    "turns wo:1 u0:2 u1:1",
    "d2:1 d1:1 d3:0 d0:0",
    "summary wo:2 u0:3 d3:1",
    "d0:1 u1:2 near20 d2:2",
    "near21 d1:2 near10 wo:3",
    "memory u0:4 near11 near30",
    "d3:2 d0:2 near31 near01",
    "u1:3 d2:3 d1:3 d3:3",
    "bank_b near00 d0:3 u1:4",
    "bank_c far20 d2:4 far21",
    "far10 far11 d1:4 far30",
    "far31 far01 d3:4 far00",
    "d0:4 mix norm_two up00",
    "up01 u0:5 up02 up03",
    "up10 up11 u1:5 up12",
    "up13 d2:5 down2 d1:5",
    "down1 d3:5 down3 d0:5",
    "down0",
)


def dot(a, b):
    return jnp.dot(a, b, preferred_element_type=F32)


def normalize(x, gain):
    mean = jnp.sum(x, -1, keepdims=True) * (1.0 / D)
    square = jnp.sum(x * x, -1, keepdims=True) * (1.0 / D)
    return (x - mean) * lax.rsqrt(square - mean * mean + EPS) * gain


def kernel(
    valid, g1, g2, frames, wq, wk, wv, wo, up, dn, out,
    xs, nrm, wqkv, sums, qb, kb, vb, kt, look_out, look_in, so_all, bank, memf, bk, bv,
    wo_b, up_b, dn_b, acc, mx, fo_out, fo_in, mixed, n2, hid, ob,
    loc_sem, send_sem, recv_sem,
):
    tm = lax.axis_index("tm")
    mp = lax.axis_index("mp")
    x = tm // 8
    y = (tm // 2) % 4
    zl = mp // 2
    z = (tm % 2) * 4 + zl
    c = mp % 2
    valid_at = lambda which: valid[which] - tm * SPAN

    def dev(px, py, pz, pc):
        return ((px * 4 + py) * 2 + pz // 4, (pz % 4) * 2 + pc)

    def z_dev(step):
        return dev(x, y, (z + step + 8) % 8, c)

    sibling = (tm, zl * 2 + 1 - c)

    barrier = pltpu.get_barrier_semaphore()

    before, after = ((tm + 31) % 32, mp), ((tm + 1) % 32, mp)
    greeted = [before, after] + [z_dev(step) for step in (1, -1, 2, -2)]
    greeted += [(tm, (mp + i) % 8) for i in range(1, 8)]
    bank_one = [dev((x + i) % 4, y, (z + j) % 8, c) for j in (4, 0) for i in (2, 1, 3, 0) if i or j]
    bank_two = [dev(x, (y + i) % 4, z, c) for i in (2, 1, 3)]
    greeted += bank_one + bank_two
    for other in greeted:
        pl.semaphore_signal(barrier, inc=1, device_id=other, device_id_type=MESH)

    used = [0]
    sent = []

    def remote(src, dst, to):
        i = used[0]
        used[0] += 1
        copy = pltpu.make_async_remote_copy(
            src_ref=src, dst_ref=dst, send_sem=send_sem.at[i], recv_sem=recv_sem.at[i],
            device_id=to, device_id_type=MESH,
        )
        sent.append(copy)
        copy.start()
        return copy

    n_local = [0]

    def local(src, dst):
        i = n_local[0]
        n_local[0] += 1
        copy = pltpu.make_async_copy(src, dst, loc_sem.at[i])
        copy.start()
        return copy

    xs_copies = [local(frames.at[b], xs.at[b]) for b in range(4)]
    w_copies = [
        local(ref, wqkv.at[:, pl.ds(i * 128, 128)]) for i, ref in enumerate((wq, wk, wv))
    ]
    own_copies = [local(wo, wo_b.at[0, 0])]
    for j in range(2):
        own_copies.append(local(up.at[:, pl.ds(j * 256, 256)], up_b.at[j, 0, 0]))

    def q_cols(step):
        return pl.ds(pl.multiple_of(((zl + step) % 4) * 256, 256), 256)

    for r in range(4):
        own_copies.append(local(dn.at[:, q_cols(r)], dn_b.at[r, 0, 0]))

    lx = (x + c) % 4
    ly = (y + c) % 4

    def at_x(label):
        return dev((label + 4 - c) % 4, y, z, c)

    def at_y(label):
        return dev(x, (label + 4 - c) % 4, z, c)

    def first(label):
        return label + 1 - 2 * (label % 2)

    def second(label):
        return 3 - label

    class Half:
        def __init__(self, kind, source, view, base, rows):
            self.source, self.view, self.base, self.rows = source, view, base, rows
            if kind == 0:
                self.a, self.b, self.at_a, self.at_b = lx, ly, at_x, at_y
            else:
                self.a, self.b, self.at_a, self.at_b = ly, lx, at_y, at_x
            self.far = 2 if kind == 0 else -2

        def span(self, index, count):
            return pl.ds(pl.multiple_of(self.base + index * self.rows, self.rows), count * self.rows)

        def z(self):
            here = self.span(self.b * 4 + self.a, 1)
            self.arrive = [
                remote(self.source(1, here), self.view(0, pl.ds(3, 1), here), z_dev(1)),
                remote(self.source(-1, here), self.view(0, pl.ds(1, 1), here), z_dev(-1)),
                remote(self.source(self.far, here), self.view(0, pl.ds(2, 1), here), z_dev(self.far)),
            ]

        def hop(self, rows, to):
            for copy in self.arrive:
                copy.wait_recv()
            part = self.view(0, pl.ds(1, 3), rows)
            self.arrive = [remote(part, part, to)]

        def s1(self):
            for copy in self.arrive:
                copy.wait_recv()
            part = self.view(0, pl.ds(1, 3), self.span(self.b * 4 + self.a, 1))
            self.arrive = [remote(part, part, self.at_a((self.a + i) % 4)) for i in (2, 1, 3)]

        def s2(self):
            self.hop(self.span(self.b * 4, 4), self.at_b(first(self.b)))

        def s3(self):
            near = self.span(8 * (self.b // 2), 8)
            self.hop(near, self.at_b(second(self.b)))
            self.share = [
                remote(self.view(0, pl.ds(1, 3), near), self.view(1, pl.ds(1, 3), near), sibling)
            ]

        def s4(self):
            for copy in self.arrive:
                copy.wait_recv()
            rest = self.span(8 - 8 * (self.b // 2), 8)
            self.share.append(
                remote(self.view(0, pl.ds(1, 3), rest), self.view(1, pl.ds(1, 3), rest), sibling)
            )

        def s5(self):
            for copy in self.share:
                copy.wait_recv()

    class Group:
        def __init__(self, halves, own, own_src):
            self.halves = halves
            self.own, self.own_src = own, own_src

        def z(self):
            for half in self.halves:
                half.z()
            self.own_copies = [
                remote(src, dst.at[pl.ds(1, 1), pl.ds(0, 1)], sibling)
                for src, dst in zip(self.own_src, self.own)
            ]

        def run(self, stage):
            if stage == 0:
                return self.z()
            for half in self.halves:
                getattr(half, "s%d" % stage)()
            if stage == 5:
                for copy in self.own_copies:
                    copy.wait_recv()

    def four(ref, rows, columns):
        return ref.reshape(1, 1, rows, columns)

    def half_up(kind, j):
        return Half(
            kind,
            lambda step, rows: four(up, D, 512).at[0, :, rows, pl.ds(j * 256, 256)],
            lambda e, d, rows: up_b.at[j, e, d, rows, :],
            kind * 512, 32,
        )

    def half_dn(kind, r):
        return Half(
            kind,
            lambda step, rows: four(dn, 512, D).at[0, :, rows, q_cols(r + step + 4)],
            lambda e, d, rows: dn_b.at[r, e, d, rows, :],
            kind * 256, 16,
        )

    groups = {}
    for j in range(2):
        groups["u%d" % j] = Group(
            [half_up(0, j), half_up(1, j)], [up_b.at[j]],
            [four(up, D, 512).at[:, :, :, pl.ds(j * 256, 256)]],
        )
    for r in range(4):
        groups["d%d" % r] = Group(
            [half_dn(0, r), half_dn(1, r)], [dn_b.at[r]],
            [four(dn, 512, D).at[:, :, :, q_cols(r)]],
        )

    class Ring:
        def __init__(self, ref, buf, rows):
            self.ref, self.buf, self.rows = ref, buf, rows

        def run(self, stage):
            buf, half = self.buf, self.rows // 2
            if stage == 0:
                self.up = remote(self.ref, buf.at[0, 3], z_dev(1))
                self.down = remote(self.ref, buf.at[0, 1], z_dev(-1))
                self.share = [remote(self.ref, buf.at[1, 0], sibling)]
            elif stage == 1:
                self.up.wait_recv()
                self.down.wait_recv()
                high, low = pl.ds(half, half), pl.ds(0, half)
                self.far = [
                    remote(buf.at[0, 3, high], buf.at[0, 2, high], z_dev(1)),
                    remote(buf.at[0, 1, low], buf.at[0, 2, low], z_dev(-1)),
                ]
                self.share.append(remote(buf.at[0, 1], buf.at[1, 1], sibling))
                self.share.append(remote(buf.at[0, 3], buf.at[1, 3], sibling))
            elif stage == 2:
                for copy in self.far:
                    copy.wait_recv()
                self.share.append(remote(buf.at[0, 2], buf.at[1, 2], sibling))
            else:
                for copy in self.share:
                    copy.wait_recv()

    groups["wo"] = Ring(wo, wo_b, 128)

    acts = {}

    def action(f):
        acts[f.__name__] = f
        return f

    def loop(f, lo, hi, unroll=1):
        lax.fori_loop(lo, hi, lambda i, carry: (f(i), carry)[1], 0, unroll=unroll)

    @action
    def enter():
        pl.semaphore_wait(barrier, len(greeted))

    held = {}

    def pre(n):
        b, half = n // 2, n % 2
        if n == 0:
            for copy in w_copies:
                copy.wait()
        if half == 0:
            xs_copies[b].wait()

        def norm_rows(i):
            rows = pl.ds(pl.multiple_of(half * OWN + i * 32, 32), 32)
            here = pl.ds(pl.multiple_of(i * 32, 32), 32)
            nrm[n % 2, here, :] = normalize(xs[b, rows, :].astype(F32), g1[...]).astype(BF16)

        loop(norm_rows, 0, 10, unroll=2)
        normed = nrm[n % 2]
        got = dot(normed, wqkv[...])
        rows = slice(half * OWN, half * OWN + OWN)
        qb[b, rows] = got[:, :128].astype(BF16) * jnp.asarray(0.125, BF16)
        kb[b, rows] = got[:, 128:256]
        vb[b, rows] = got[:, 256:].astype(BF16)
        if half == 0:
            look_out[b] = got[:LOOK, 128:].astype(BF16)
        row_i = lax.broadcasted_iota(jnp.int32, (16, OWN), 0)
        col_i = lax.broadcasted_iota(jnp.int32, (16, OWN), 1)
        live = col_i < valid_at(b) - half * OWN
        inside = (col_i >= row_i * SEG) & (col_i < row_i * SEG + SEG) & live
        picks = jnp.where(inside, 1.0, 0.0)
        counts = jnp.sum(picks, -1, keepdims=True)
        total = dot(picks.astype(BF16), normed) / jnp.maximum(counts, 1.0)
        sums[2 * n : 2 * n + 2, :] = total[:2]

    for n in range(8):
        acts["pre%d" % n] = lambda n=n: pre(n)

    @action
    def look():
        held["look"] = remote(look_out, look_in, before)

    def turn(b):
        for sl in range(4):
            kt[b * 4 + sl] = kb[b, sl * SEG : sl * SEG + KEYS].T.astype(BF16)

    @action
    def turns():
        held["look"].wait_recv()
        for b in range(4):
            kb[b, SPAN:] = look_in[b, :, :128].astype(F32)
            vb[b, SPAN:] = look_in[b, :, 128:]
        for copy in own_copies:
            copy.wait()
        loop(turn, 0, 4)

    @action
    def summary():
        asked = dot(sums[...].astype(BF16), wqkv[:, :128]).astype(BF16).astype(F32) * 0.125
        row = lax.broadcasted_iota(jnp.int32, (8, 128), 0)
        head = lax.broadcasted_iota(jnp.int32, (8, 128), 1) // 64
        key_l = lax.broadcasted_iota(jnp.int32, (8, KEYS), 1)
        parts = []
        for g in range(16):
            q = jnp.where(row == head, jnp.broadcast_to(asked[g : g + 1], (8, 128)), 0.0)
            score = dot(q.astype(BF16), kt[g])
            parts.append(jnp.where(key_l < valid_at(g // 4) - (g % 4) * SEG, score, NEG))
        scores = jnp.concatenate(parts, axis=0)
        p = jnp.exp(scores - jnp.max(scores, -1, keepdims=True))
        p = p / jnp.sum(p, -1, keepdims=True)
        parts = []
        for g in range(16):
            at = (g % 4) * SEG
            got = dot(p[g * 8 : g * 8 + 8].astype(BF16), vb[g // 4, at : at + KEYS, :])
            parts.append(jnp.where(head[:1] == 0, got[0:1], got[1:2]))
        so_all[0, 0] = jnp.concatenate(parts, axis=0).astype(BF16)
        held["so"] = []
        for dz in (2, 3, 1, 0):
            for e in range(2):
                if dz or e:
                    to = (tm, ((zl + dz) % 4) * 2 + (c if e == 0 else 1 - c))
                    held["so"].append(remote(so_all.at[0, 0], so_all.at[e, (4 - dz) % 4], to))

    zh = tm % 2

    @action
    def memory():
        for copy in held["so"]:
            copy.wait_recv()
        summed = jnp.concatenate([so_all[e, d] for e in range(2) for d in range(4)], axis=1)
        got = dot(summed, wo_b[...].reshape(D, D)).astype(BF16)
        bank[x, y, zh] = dot(got, wqkv[:, 128:]).astype(BF16)
        part = bank.at[x, y, zh]
        held["bank"] = [remote(part, part, other) for other in bank_one]

    @action
    def bank_b():
        for copy in held["bank"]:
            copy.wait_recv()
        part = bank.at[:, pl.ds(y, 1)]
        held["bank"] = [remote(part, part, other) for other in bank_two]

    @action
    def bank_c():
        for copy in held["bank"]:
            copy.wait_recv()
        memf[0] = bank[:, :, :, :, :128].reshape(SLOTS * 4, 128).astype(F32)
        memf[1] = bank[:, :, :, :, 128:].reshape(SLOTS * 4, 128).astype(F32)
        for b in range(4):
            both = [
                jnp.concatenate(
                    [memf[i, pl.ds(b * 4 + sl, 32, stride=16), :] for sl in range(4)], axis=0
                )
                for i in range(2)
            ]
            bk[b] = both[0].T.astype(BF16)
            bv[b] = both[1].astype(BF16)

    lane = lax.broadcasted_iota(jnp.int32, (SEG, 128), 1)

    def one_head(b, seg, h):
        q = qb[b, pl.ds(pl.multiple_of(seg * SEG, 32), SEG), :]
        mine = lane < 64 if h == 0 else lane >= 64
        return jnp.where(mine, q, jnp.zeros_like(q))

    def with_ones(v):
        return jnp.concatenate([v, jnp.ones_like(v)], axis=1)

    def near_step(b, seg):
        g = b * 4 + seg
        near_l = lax.broadcasted_iota(jnp.int32, (SEG, KEYS), 1)
        ones = with_ones(vb[b, pl.ds(pl.multiple_of(seg * SEG, 32), KEYS), :])
        for h in range(2):
            near = dot(one_head(b, seg, h), kt[g])
            near = jnp.where(near_l < valid_at(b) - seg * SEG, near, NEG)
            top = jnp.max(near, -1, keepdims=True)
            near = jnp.exp(near - top).astype(BF16)
            rows = slice(h * SEG, h * SEG + SEG)
            acc[g, rows] = dot(near, ones)
            mx[g, rows] = jnp.broadcast_to(top, (SEG, 128))

    def far_step(b, seg, s, dest):
        g = b * 4 + seg
        far_l = lax.broadcasted_iota(jnp.int32, (SEG, SLOTS), 1)
        far_l = (far_l % 32) * 4 + far_l // 32
        far_ok = (far_l < tm * 4 + seg) & (far_l * SEG < valid[b])
        both = []
        for h in range(2):
            rows = slice(h * SEG, h * SEG + SEG)
            far = jnp.where(far_ok, dot(one_head(b, seg, h), bk[b]), NEG)
            before = mx[g, rows]
            top = jnp.maximum(before, jnp.max(far, -1, keepdims=True))
            far = jnp.exp(far - top).astype(BF16)
            keep = jnp.exp(before - top)
            got = dot(far, with_ones(bv[b]))
            total = acc[g, rows, 128:] * keep + got[:, 128:]
            both.append((acc[g, rows, :128] * keep + got[:, :128]) / total)
        dest[s * SEG : s * SEG + SEG, :] = jnp.where(lane < 64, both[0], both[1]).astype(BF16)

    def place(r, i):
        return (zl + r) % 4, (c if i == 0 else 1 - c)

    def near(r, i):
        b, core = place(r, i)
        for s in range(2):
            near_step(b, core * 2 + s)

    held["fo"] = []

    def far(r, i):
        b, core = place(r, i)
        dest = fo_out.at[r, i] if r or i else fo_in.at[0, 0]
        for s in range(2):
            far_step(b, core * 2 + s, s, dest)
        if r or i:
            held["fo"].append(remote(dest, fo_in.at[i, (4 - r) % 4], (tm, b * 2 + core)))

    for r in range(4):
        for i in range(2):
            acts["near%d%d" % (r, i)] = lambda r=r, i=i: near(r, i)
            acts["far%d%d" % (r, i)] = lambda r=r, i=i: far(r, i)

    @action
    def mix():
        for copy in held["fo"]:
            copy.wait_recv()
        rows = jnp.concatenate([fo_in[e, d] for e in range(2) for d in range(4)], axis=1)
        own = pl.ds(pl.multiple_of(c * OWN, OWN), OWN)
        for n in range(4):
            weight = wo_b[:, :, :, n * 256 : n * 256 + 256].reshape(D, 256)
            mixed[n] = dot(rows, weight) + xs[zl, own, n * 256 : n * 256 + 256].astype(F32)

    @action
    def norm_two():
        def step(i):
            rows = pl.ds(pl.multiple_of(i * 32, 32), 32)
            v = jnp.concatenate([mixed[n, rows, :] for n in range(4)], axis=1)
            n2[rows, :] = normalize(v, g2[...]).astype(BF16)

        loop(step, 0, 10, unroll=2)

    def up_step(j, b):
        h = dot(n2[...], up_b[j, b // 4, b % 4])
        h = 0.5 * h * (1.0 + lax.erf(h * (2.0 ** -0.5)))
        hid[:, pl.ds(pl.multiple_of(b * 512 + j * 256, 256), 256)] = h.astype(BF16)

    for j in range(2):
        for k in range(4):
            acts["up%d%d" % (j, k)] = lambda j=j, k=k: loop(
                lambda b: up_step(j, b), 2 * k, 2 * k + 2)

    outs = []
    row_span = pl.ds(pl.multiple_of(c * OWN, OWN), OWN)

    def down(r):
        block = dot(hid[...], dn_b[r].reshape(4 * D, 256))
        to = (zl + r) % 4
        block = (block + mixed[to]).astype(BF16)
        ob[r, 0] = block[:, :128]
        ob[r, 1] = block[:, 128:]
        if r:
            for core in (c, 1 - c):
                outs.append(remote(ob.at[r, core], out.at[zl, row_span, :], (tm, to * 2 + core)))
        else:
            outs.append(remote(ob.at[0, 1 - c], out.at[zl, row_span, :], sibling))
            held["home"] = local(ob.at[0, c], out.at[zl, row_span, :])

    for r in range(4):
        acts["down%d" % r] = lambda r=r: down(r)

    for token in " ".join(SCHEDULE).split():
        if ":" in token:
            name, stage = token.split(":")
            groups[name].run(int(stage))
        else:
            acts[token]()
    held["home"].wait()
    for copy in outs:
        copy.wait_recv()
    for copy in sent:
        copy.wait_send()
    assert used[0] <= N_SEM, used[0]


def body(frames, valid, ln1_gain, w_query, w_key, w_value, w_out, ln2_gain, w_up, w_down):
    vmem = pl.BlockSpec(memory_space=pltpu.VMEM)
    anywhere = pl.BlockSpec(memory_space=pl.ANY)
    scratch = [
        pltpu.VMEM((4, SPAN, D), BF16),
        pltpu.VMEM((2, OWN, D), BF16),
        pltpu.VMEM((D, 384), BF16),
        pltpu.VMEM((16, D), F32),
        pltpu.VMEM((4, SPAN, 128), BF16),
        pltpu.VMEM((4, SPAN + LOOK, 128), F32),
        pltpu.VMEM((4, SPAN + LOOK, 128), BF16),
        pltpu.VMEM((16, 128, KEYS), BF16),
        pltpu.VMEM((4, LOOK, 256), BF16),
        pltpu.VMEM((4, LOOK, 256), BF16),
        pltpu.VMEM((2, 4, 16, 128), BF16),
        pltpu.VMEM((4, 4, 2, 16, 256), BF16),
        pltpu.VMEM((2, SLOTS * 4, 128), F32),
        pltpu.VMEM((4, 128, SLOTS), BF16),
        pltpu.VMEM((4, SLOTS, 128), BF16),
        pltpu.VMEM((2, 4, 128, D), BF16),
        pltpu.VMEM((2, 2, 4, D, 256), BF16),
        pltpu.VMEM((4, 2, 4, 512, 256), BF16),
        pltpu.VMEM((16, OWN, 256), F32),
        pltpu.VMEM((16, OWN, 128), F32),
        pltpu.VMEM((4, 2, OWN, 128), BF16),
        pltpu.VMEM((2, 4, OWN, 128), BF16),
        pltpu.VMEM((4, OWN, 256), F32),
        pltpu.VMEM((OWN, D), BF16),
        pltpu.VMEM((OWN, 4 * D), BF16),
        pltpu.VMEM((4, 2, OWN, 128), BF16),
        pltpu.SemaphoreType.DMA((16,)),
        pltpu.SemaphoreType.DMA((N_SEM,)),
        pltpu.SemaphoreType.DMA((N_SEM,)),
    ]
    return pl.pallas_call(
        kernel,
        name="layer",
        out_shape=jax.ShapeDtypeStruct((frames.shape[0], frames.shape[1], 128), BF16),
        in_specs=[pl.BlockSpec(memory_space=pltpu.SMEM), vmem, vmem] + [anywhere] * 7,
        out_specs=anywhere,
        scratch_shapes=scratch,
        compiler_params=pltpu.CompilerParams(
            collective_id=0, has_side_effects=True, vmem_limit_bytes=56 * 2**20
        ),
    )(
        valid, ln1_gain.reshape(1, D), ln2_gain.reshape(1, D),
        frames, w_query, w_key, w_value, w_out, w_up, w_down,
    )


def solution(mesh):
    placed = (
        P(None, "tm", None),
        P(),
        P(),
        P(None, "mp"),
        P(None, "mp"),
        P(None, "mp"),
        P("mp", None),
        P(),
        P(None, "mp"),
        P("mp", None),
    )
    return jax.shard_map(
        body, mesh=mesh, in_specs=placed, out_specs=P(None, "tm", "mp"), check_vma=False
    )
```

```python
import jax
import jax.numpy as jnp
from jax import lax
from jax.experimental import pallas as pl
from jax.experimental.pallas import tpu as pltpu
from jax.sharding import PartitionSpec as P

MESH = pl.DeviceIdType.MESH
F32 = jnp.float32
BF16 = jnp.bfloat16

D = 1024
SEG = 160
LOOK = 32
KEYS = SEG + LOOK
OWN = 2 * SEG
SPAN = 4 * SEG
SLOTS = 128
EPS = 1e-05
NEG = -1e30
N_SEM = 192

SCHEDULE = (
    "pre0 pre2 pre4 pre6",
    "enter u0:0 wo:0 look",
    "pre1 pre3 u1:0 pre5",
    "pre7 d2:0 wo:1 u0:1",
    "turns summary near20 d1:0",
    "wo:2 near21 near10 near11",
    "u1:1 d2:1 d3:0 wo:3",
    "memory u0:2 near30 d0:0",
    "near31 d1:1 near01 u1:2",
    "d3:1 bank_b d2:2 near00",
    "u0:3 d0:1 d1:2 bank_c",
    "far200 far210 far100 far110",
    "u1:3 far300 far310 far010",
    "d3:2 far000 d2:3 far201",
    "far211 far101 far111 far301",
    "far311 far011 far001 u0:4",
    "d0:2 d1:3 mix0 norm0",
    "u1:4 up000 up010 d3:3",
    "u0:5 up020 up030 up100",
    "d2:4 up110 u1:5 up120",
    "d0:3 up130 d2:5 down20",
    "d1:4 d1:5 down10 d3:4",
    "d3:5 down30 d0:4 d0:5",
    "down00 mix1 norm1 up001",
    "up011 up021 up031 up101",
    "up111 up121 up131 down21",
    "down11 down31 down01",
)


def dot(a, b):
    return jnp.dot(a, b, preferred_element_type=F32)


def normalize(x, gain):
    mean = jnp.sum(x, -1, keepdims=True) * (1.0 / D)
    square = jnp.sum(x * x, -1, keepdims=True) * (1.0 / D)
    return (x - mean) * lax.rsqrt(square - mean * mean + EPS) * gain


def kernel(
    valid, g1, g2, frames, wq, wk, wv, wo, up, dn, out,
    xs, nrm, wqkv, sums, qb, kb, vb, kt, look_out, look_in, so_all, bank, memf, bk, bv,
    wo_b, up_b, dn_b, acc, mx, fo_out, fo_in, mixed, n2, hid, ob,
    loc_sem, send_sem, recv_sem,
):
    tm = lax.axis_index("tm")
    mp = lax.axis_index("mp")
    x = tm // 8
    y = (tm // 2) % 4
    zl = mp // 2
    z = (tm % 2) * 4 + zl
    c = mp % 2
    valid_at = lambda which: valid[which] - tm * SPAN

    def dev(px, py, pz, pc):
        return ((px * 4 + py) * 2 + pz // 4, (pz % 4) * 2 + pc)

    def z_dev(step):
        return dev(x, y, (z + step + 8) % 8, c)

    sibling = (tm, zl * 2 + 1 - c)

    barrier = pltpu.get_barrier_semaphore()

    before, after = ((tm + 31) % 32, mp), ((tm + 1) % 32, mp)
    greeted = [before, after] + [z_dev(step) for step in (1, -1, 2, -2)]
    greeted += [(tm, (mp + i) % 8) for i in range(1, 8)]
    bank_one = [dev((x + i) % 4, y, (z + j) % 8, c) for j in (4, 0) for i in (2, 1, 3, 0) if i or j]
    bank_two = [dev(x, (y + i) % 4, z, c) for i in (2, 1, 3)]
    greeted += bank_one + bank_two
    for other in greeted:
        pl.semaphore_signal(barrier, inc=1, device_id=other, device_id_type=MESH)

    used = [0]
    sent = []

    def remote(src, dst, to):
        i = used[0]
        used[0] += 1
        copy = pltpu.make_async_remote_copy(
            src_ref=src, dst_ref=dst, send_sem=send_sem.at[i], recv_sem=recv_sem.at[i],
            device_id=to, device_id_type=MESH,
        )
        sent.append(copy)
        copy.start()
        return copy

    n_local = [0]

    def local(src, dst):
        i = n_local[0]
        n_local[0] += 1
        copy = pltpu.make_async_copy(src, dst, loc_sem.at[i])
        copy.start()
        return copy

    xs_copies = [local(frames.at[b], xs.at[b]) for b in range(4)]
    w_copies = [
        local(ref, wqkv.at[:, pl.ds(i * 128, 128)]) for i, ref in enumerate((wq, wk, wv))
    ]
    own_copies = [local(wo, wo_b.at[0, 0])]
    for j in range(2):
        own_copies.append(local(up.at[:, pl.ds(j * 256, 256)], up_b.at[j, 0, 0]))

    def q_cols(step):
        return pl.ds(pl.multiple_of(((zl + step) % 4) * 256, 256), 256)

    for r in range(4):
        own_copies.append(local(dn.at[:, q_cols(r)], dn_b.at[r, 0, 0]))

    lx = (x + c) % 4
    ly = (y + c) % 4

    def at_x(label):
        return dev((label + 4 - c) % 4, y, z, c)

    def at_y(label):
        return dev(x, (label + 4 - c) % 4, z, c)

    def first(label):
        return label + 1 - 2 * (label % 2)

    def second(label):
        return 3 - label

    class Half:
        def __init__(self, kind, source, view, base, rows):
            self.source, self.view, self.base, self.rows = source, view, base, rows
            if kind == 0:
                self.a, self.b, self.at_a, self.at_b = lx, ly, at_x, at_y
            else:
                self.a, self.b, self.at_a, self.at_b = ly, lx, at_y, at_x
            self.far = 2 if kind == 0 else -2

        def span(self, index, count):
            return pl.ds(pl.multiple_of(self.base + index * self.rows, self.rows), count * self.rows)

        def z(self):
            here = self.span(self.b * 4 + self.a, 1)
            self.arrive = [
                remote(self.source(1, here), self.view(0, pl.ds(3, 1), here), z_dev(1)),
                remote(self.source(-1, here), self.view(0, pl.ds(1, 1), here), z_dev(-1)),
                remote(self.source(self.far, here), self.view(0, pl.ds(2, 1), here), z_dev(self.far)),
            ]

        def hop(self, rows, to):
            for copy in self.arrive:
                copy.wait_recv()
            part = self.view(0, pl.ds(1, 3), rows)
            self.arrive = [remote(part, part, to)]

        def s1(self):
            for copy in self.arrive:
                copy.wait_recv()
            part = self.view(0, pl.ds(1, 3), self.span(self.b * 4 + self.a, 1))
            self.arrive = [remote(part, part, self.at_a((self.a + i) % 4)) for i in (2, 1, 3)]

        def s2(self):
            self.hop(self.span(self.b * 4, 4), self.at_b(first(self.b)))

        def s3(self):
            near = self.span(8 * (self.b // 2), 8)
            self.hop(near, self.at_b(second(self.b)))
            self.share = [
                remote(self.view(0, pl.ds(1, 3), near), self.view(1, pl.ds(1, 3), near), sibling)
            ]

        def s4(self):
            for copy in self.arrive:
                copy.wait_recv()
            rest = self.span(8 - 8 * (self.b // 2), 8)
            self.share.append(
                remote(self.view(0, pl.ds(1, 3), rest), self.view(1, pl.ds(1, 3), rest), sibling)
            )

        def s5(self):
            for copy in self.share:
                copy.wait_recv()

    class Group:
        def __init__(self, halves, own, own_src):
            self.halves = halves
            self.own, self.own_src = own, own_src

        def z(self):
            for half in self.halves:
                half.z()
            self.own_copies = [
                remote(src, dst.at[pl.ds(1, 1), pl.ds(0, 1)], sibling)
                for src, dst in zip(self.own_src, self.own)
            ]

        def run(self, stage):
            if stage == 0:
                return self.z()
            for half in self.halves:
                getattr(half, "s%d" % stage)()
            if stage == 5:
                for copy in self.own_copies:
                    copy.wait_recv()

    def four(ref, rows, columns):
        return ref.reshape(1, 1, rows, columns)

    def half_up(kind, j):
        return Half(
            kind,
            lambda step, rows: four(up, D, 512).at[0, :, rows, pl.ds(j * 256, 256)],
            lambda e, d, rows: up_b.at[j, e, d, rows, :],
            kind * 512, 32,
        )

    def half_dn(kind, r):
        return Half(
            kind,
            lambda step, rows: four(dn, 512, D).at[0, :, rows, q_cols(r + step + 4)],
            lambda e, d, rows: dn_b.at[r, e, d, rows, :],
            kind * 256, 16,
        )

    groups = {}
    for j in range(2):
        groups["u%d" % j] = Group(
            [half_up(0, j), half_up(1, j)], [up_b.at[j]],
            [four(up, D, 512).at[:, :, :, pl.ds(j * 256, 256)]],
        )
    for r in range(4):
        groups["d%d" % r] = Group(
            [half_dn(0, r), half_dn(1, r)], [dn_b.at[r]],
            [four(dn, 512, D).at[:, :, :, q_cols(r)]],
        )

    class Ring:
        def __init__(self, ref, buf, rows):
            self.ref, self.buf, self.rows = ref, buf, rows

        def run(self, stage):
            buf, half = self.buf, self.rows // 2
            if stage == 0:
                self.up = remote(self.ref, buf.at[0, 3], z_dev(1))
                self.down = remote(self.ref, buf.at[0, 1], z_dev(-1))
                self.share = [remote(self.ref, buf.at[1, 0], sibling)]
            elif stage == 1:
                self.up.wait_recv()
                self.down.wait_recv()
                high, low = pl.ds(half, half), pl.ds(0, half)
                self.far = [
                    remote(buf.at[0, 3, high], buf.at[0, 2, high], z_dev(1)),
                    remote(buf.at[0, 1, low], buf.at[0, 2, low], z_dev(-1)),
                ]
                self.share.append(remote(buf.at[0, 1], buf.at[1, 1], sibling))
                self.share.append(remote(buf.at[0, 3], buf.at[1, 3], sibling))
            elif stage == 2:
                for copy in self.far:
                    copy.wait_recv()
                self.share.append(remote(buf.at[0, 2], buf.at[1, 2], sibling))
            else:
                for copy in self.share:
                    copy.wait_recv()

    groups["wo"] = Ring(wo, wo_b, 128)

    acts = {}

    def action(f):
        acts[f.__name__] = f
        return f

    def loop(f, lo, hi, unroll=1):
        lax.fori_loop(lo, hi, lambda i, carry: (f(i), carry)[1], 0, unroll=unroll)

    @action
    def enter():
        pl.semaphore_wait(barrier, len(greeted))

    held = {}

    def pre(n):
        b, half = n // 2, n % 2
        if n == 0:
            for copy in w_copies:
                copy.wait()
        if half == 0:
            xs_copies[b].wait()

        def norm_rows(i):
            rows = pl.ds(pl.multiple_of(half * OWN + i * 32, 32), 32)
            here = pl.ds(pl.multiple_of(i * 32, 32), 32)
            nrm[n % 2, here, :] = normalize(xs[b, rows, :].astype(F32), g1[...]).astype(BF16)

        loop(norm_rows, 0, 10, unroll=2)
        normed = nrm[n % 2]
        got = dot(normed, wqkv[...])
        rows = slice(half * OWN, half * OWN + OWN)
        qb[b, rows] = got[:, :128].astype(BF16) * jnp.asarray(0.125, BF16)
        kb[b, rows] = got[:, 128:256]
        vb[b, rows] = got[:, 256:].astype(BF16)
        if half == 0:
            look_out[b] = got[:LOOK, 128:].astype(BF16)
        row_i = lax.broadcasted_iota(jnp.int32, (16, OWN), 0)
        col_i = lax.broadcasted_iota(jnp.int32, (16, OWN), 1)
        live = col_i < valid_at(b) - half * OWN
        inside = (col_i >= row_i * SEG) & (col_i < row_i * SEG + SEG) & live
        picks = jnp.where(inside, 1.0, 0.0)
        counts = jnp.sum(picks, -1, keepdims=True)
        total = dot(picks.astype(BF16), normed) / jnp.maximum(counts, 1.0)
        sums[2 * n : 2 * n + 2, :] = total[:2]

    for n in range(8):
        acts["pre%d" % n] = lambda n=n: pre(n)

    @action
    def look():
        held["look"] = remote(look_out, look_in, before)

    def turn(b):
        for sl in range(4):
            kt[b * 4 + sl] = kb[b, sl * SEG : sl * SEG + KEYS].T.astype(BF16)

    @action
    def turns():
        held["look"].wait_recv()
        for b in range(4):
            kb[b, SPAN:] = look_in[b, :, :128].astype(F32)
            vb[b, SPAN:] = look_in[b, :, 128:]
        for copy in own_copies:
            copy.wait()
        loop(turn, 0, 4)

    @action
    def summary():
        asked = dot(sums[...].astype(BF16), wqkv[:, :128]).astype(BF16).astype(F32) * 0.125
        row = lax.broadcasted_iota(jnp.int32, (8, 128), 0)
        head = lax.broadcasted_iota(jnp.int32, (8, 128), 1) // 64
        key_l = lax.broadcasted_iota(jnp.int32, (8, KEYS), 1)
        parts = []
        for g in range(16):
            q = jnp.where(row == head, jnp.broadcast_to(asked[g : g + 1], (8, 128)), 0.0)
            score = dot(q.astype(BF16), kt[g])
            parts.append(jnp.where(key_l < valid_at(g // 4) - (g % 4) * SEG, score, NEG))
        scores = jnp.concatenate(parts, axis=0)
        p = jnp.exp(scores - jnp.max(scores, -1, keepdims=True))
        p = p / jnp.sum(p, -1, keepdims=True)
        parts = []
        for g in range(16):
            at = (g % 4) * SEG
            got = dot(p[g * 8 : g * 8 + 8].astype(BF16), vb[g // 4, at : at + KEYS, :])
            parts.append(jnp.where(head[:1] == 0, got[0:1], got[1:2]))
        so_all[0, 0] = jnp.concatenate(parts, axis=0).astype(BF16)
        held["so"] = []
        for dz in (2, 3, 1, 0):
            for e in range(2):
                if dz or e:
                    to = (tm, ((zl + dz) % 4) * 2 + (c if e == 0 else 1 - c))
                    held["so"].append(remote(so_all.at[0, 0], so_all.at[e, (4 - dz) % 4], to))

    zh = tm % 2

    @action
    def memory():
        for copy in held["so"]:
            copy.wait_recv()
        summed = jnp.concatenate([so_all[e, d] for e in range(2) for d in range(4)], axis=1)
        got = dot(summed, wo_b[...].reshape(D, D)).astype(BF16)
        bank[x, y, zh] = dot(got, wqkv[:, 128:]).astype(BF16)
        part = bank.at[x, y, zh]
        held["bank"] = [remote(part, part, other) for other in bank_one]

    @action
    def bank_b():
        for copy in held["bank"]:
            copy.wait_recv()
        part = bank.at[:, pl.ds(y, 1)]
        held["bank"] = [remote(part, part, other) for other in bank_two]

    @action
    def bank_c():
        for copy in held["bank"]:
            copy.wait_recv()
        memf[0] = bank[:, :, :, :, :128].reshape(SLOTS * 4, 128).astype(F32)
        memf[1] = bank[:, :, :, :, 128:].reshape(SLOTS * 4, 128).astype(F32)
        for b in range(4):
            both = [
                jnp.concatenate(
                    [memf[i, pl.ds(b * 4 + sl, 32, stride=16), :] for sl in range(4)], axis=0
                )
                for i in range(2)
            ]
            bk[b] = both[0].T.astype(BF16)
            bv[b] = both[1].astype(BF16)

    lane = lax.broadcasted_iota(jnp.int32, (SEG, 128), 1)

    def one_head(b, seg, h):
        q = qb[b, pl.ds(pl.multiple_of(seg * SEG, 32), SEG), :]
        mine = lane < 64 if h == 0 else lane >= 64
        return jnp.where(mine, q, jnp.zeros_like(q))

    def with_ones(v):
        return jnp.concatenate([v, jnp.ones_like(v)], axis=1)

    def near_step(b, seg):
        g = b * 4 + seg
        near_l = lax.broadcasted_iota(jnp.int32, (SEG, KEYS), 1)
        ones = with_ones(vb[b, pl.ds(pl.multiple_of(seg * SEG, 32), KEYS), :])
        for h in range(2):
            near = dot(one_head(b, seg, h), kt[g])
            near = jnp.where(near_l < valid_at(b) - seg * SEG, near, NEG)
            top = jnp.max(near, -1, keepdims=True)
            near = jnp.exp(near - top).astype(BF16)
            rows = slice(h * SEG, h * SEG + SEG)
            acc[g, rows] = dot(near, ones)
            mx[g, rows] = jnp.broadcast_to(top, (SEG, 128))

    def far_step(b, seg, dest):
        g = b * 4 + seg
        far_l = lax.broadcasted_iota(jnp.int32, (SEG, SLOTS), 1)
        far_l = (far_l % 32) * 4 + far_l // 32
        far_ok = (far_l < tm * 4 + seg) & (far_l * SEG < valid[b])
        both = []
        for h in range(2):
            rows = slice(h * SEG, h * SEG + SEG)
            far = jnp.where(far_ok, dot(one_head(b, seg, h), bk[b]), NEG)
            before = mx[g, rows]
            top = jnp.maximum(before, jnp.max(far, -1, keepdims=True))
            far = jnp.exp(far - top).astype(BF16)
            keep = jnp.exp(before - top)
            got = dot(far, with_ones(bv[b]))
            total = acc[g, rows, 128:] * keep + got[:, 128:]
            both.append((acc[g, rows, :128] * keep + got[:, :128]) / total)
        dest[...] = jnp.where(lane < 64, both[0], both[1]).astype(BF16)

    def place(r, i):
        return (zl + r) % 4, (c if i == 0 else 1 - c)

    def near(r, i):
        b, core = place(r, i)
        for s in range(2):
            near_step(b, core * 2 + s)

    held["fo"] = [[], []]

    def far(r, i, s):
        b, core = place(r, i)
        rows = pl.ds(s * SEG, SEG)
        if r or i:
            dest = fo_out.at[r, i, rows]
            far_step(b, core * 2 + s, dest)
            there = fo_in.at[i, (4 - r) % 4, rows]
            held["fo"][s].append(remote(dest, there, (tm, b * 2 + core)))
        else:
            far_step(b, core * 2 + s, fo_in.at[0, 0, rows])

    for r in range(4):
        for i in range(2):
            acts["near%d%d" % (r, i)] = lambda r=r, i=i: near(r, i)
            for s in range(2):
                acts["far%d%d%d" % (r, i, s)] = lambda r=r, i=i, s=s: far(r, i, s)

    def mix(s):
        for copy in held["fo"][s]:
            copy.wait_recv()
        part = slice(s * SEG, s * SEG + SEG)
        rows = jnp.concatenate([fo_in[e, d, part] for e in range(2) for d in range(4)], axis=1)
        own = pl.ds(pl.multiple_of(c * OWN + s * SEG, 32), SEG)
        for n in range(4):
            weight = wo_b[:, :, :, n * 256 : n * 256 + 256].reshape(D, 256)
            mixed[n, part] = dot(rows, weight) + xs[zl, own, n * 256 : n * 256 + 256].astype(F32)

    def norm_two(s):
        def step(i):
            rows = pl.ds(pl.multiple_of(s * SEG + i * 32, 32), 32)
            v = jnp.concatenate([mixed[n, rows, :] for n in range(4)], axis=1)
            n2[rows, :] = normalize(v, g2[...]).astype(BF16)

        loop(step, 0, 5)

    def up_step(j, b, s):
        part = slice(s * SEG, s * SEG + SEG)
        h = dot(n2[part, :], up_b[j, b // 4, b % 4])
        h = 0.5 * h * (1.0 + lax.erf(h * (2.0 ** -0.5)))
        hid[part, pl.ds(pl.multiple_of(b * 512 + j * 256, 256), 256)] = h.astype(BF16)

    for s in range(2):
        acts["mix%d" % s] = lambda s=s: mix(s)
        acts["norm%d" % s] = lambda s=s: norm_two(s)
        for j in range(2):
            for k in range(4):
                acts["up%d%d%d" % (j, k, s)] = lambda j=j, k=k, s=s: loop(
                    lambda b: up_step(j, b, s), 2 * k, 2 * k + 2, unroll=2)

    outs = []
    held["home"] = []

    def down(r, s):
        part = slice(s * SEG, s * SEG + SEG)
        rows = pl.ds(s * SEG, SEG)
        there = out.at[zl, pl.ds(pl.multiple_of(c * OWN + s * SEG, 32), SEG), :]
        block = dot(hid[part, :], dn_b[r].reshape(4 * D, 256))
        to = (zl + r) % 4
        block = (block + mixed[to, part]).astype(BF16)
        ob[r, 0, part] = block[:, :128]
        ob[r, 1, part] = block[:, 128:]
        if r:
            for core in (c, 1 - c):
                outs.append(remote(ob.at[r, core, rows], there, (tm, to * 2 + core)))
        else:
            outs.append(remote(ob.at[0, 1 - c, rows], there, sibling))
            held["home"].append(local(ob.at[0, c, rows], there))

    for r in range(4):
        for s in range(2):
            acts["down%d%d" % (r, s)] = lambda r=r, s=s: down(r, s)

    for token in " ".join(SCHEDULE).split():
        if ":" in token:
            name, stage = token.split(":")
            groups[name].run(int(stage))
        else:
            acts[token]()
    for copy in held["home"]:
        copy.wait()
    for copy in outs:
        copy.wait_recv()
    for copy in sent:
        copy.wait_send()
    assert used[0] <= N_SEM, used[0]


def body(frames, valid, ln1_gain, w_query, w_key, w_value, w_out, ln2_gain, w_up, w_down):
    vmem = pl.BlockSpec(memory_space=pltpu.VMEM)
    anywhere = pl.BlockSpec(memory_space=pl.ANY)
    scratch = [
        pltpu.VMEM((4, SPAN, D), BF16),
        pltpu.VMEM((2, OWN, D), BF16),
        pltpu.VMEM((D, 384), BF16),
        pltpu.VMEM((16, D), F32),
        pltpu.VMEM((4, SPAN, 128), BF16),
        pltpu.VMEM((4, SPAN + LOOK, 128), F32),
        pltpu.VMEM((4, SPAN + LOOK, 128), BF16),
        pltpu.VMEM((16, 128, KEYS), BF16),
        pltpu.VMEM((4, LOOK, 256), BF16),
        pltpu.VMEM((4, LOOK, 256), BF16),
        pltpu.VMEM((2, 4, 16, 128), BF16),
        pltpu.VMEM((4, 4, 2, 16, 256), BF16),
        pltpu.VMEM((2, SLOTS * 4, 128), F32),
        pltpu.VMEM((4, 128, SLOTS), BF16),
        pltpu.VMEM((4, SLOTS, 128), BF16),
        pltpu.VMEM((2, 4, 128, D), BF16),
        pltpu.VMEM((2, 2, 4, D, 256), BF16),
        pltpu.VMEM((4, 2, 4, 512, 256), BF16),
        pltpu.VMEM((16, OWN, 256), F32),
        pltpu.VMEM((16, OWN, 128), F32),
        pltpu.VMEM((4, 2, OWN, 128), BF16),
        pltpu.VMEM((2, 4, OWN, 128), BF16),
        pltpu.VMEM((4, OWN, 256), F32),
        pltpu.VMEM((OWN, D), BF16),
        pltpu.VMEM((OWN, 4 * D), BF16),
        pltpu.VMEM((4, 2, OWN, 128), BF16),
        pltpu.SemaphoreType.DMA((16,)),
        pltpu.SemaphoreType.DMA((N_SEM,)),
        pltpu.SemaphoreType.DMA((N_SEM,)),
    ]
    return pl.pallas_call(
        kernel,
        name="layer",
        out_shape=jax.ShapeDtypeStruct((frames.shape[0], frames.shape[1], 128), BF16),
        in_specs=[pl.BlockSpec(memory_space=pltpu.SMEM), vmem, vmem] + [anywhere] * 7,
        out_specs=anywhere,
        scratch_shapes=scratch,
        compiler_params=pltpu.CompilerParams(
            collective_id=0, has_side_effects=True, vmem_limit_bytes=56 * 2**20
        ),
    )(
        valid, ln1_gain.reshape(1, D), ln2_gain.reshape(1, D),
        frames, w_query, w_key, w_value, w_out, w_up, w_down,
    )


def solution(mesh):
    placed = (
        P(None, "tm", None),
        P(),
        P(),
        P(None, "mp"),
        P(None, "mp"),
        P(None, "mp"),
        P("mp", None),
        P(),
        P(None, "mp"),
        P("mp", None),
    )
    return jax.shard_map(
        body, mesh=mesh, in_specs=placed, out_specs=P(None, "tm", "mp"), check_vma=False
    )
```

```python
import jax
import jax.numpy as jnp
from jax import lax
from jax.experimental import pallas as pl
from jax.experimental.pallas import tpu as pltpu
from jax.sharding import PartitionSpec as P

MESH = pl.DeviceIdType.MESH
F32 = jnp.float32
BF16 = jnp.bfloat16

D = 1024
SEG = 160
LOOK = 32
KEYS = SEG + LOOK
OWN = 2 * SEG
SPAN = 4 * SEG
SLOTS = 128
EPS = 1e-05
NEG = -1e30
N_SEM = 192

SCHEDULE = (
    "pre0 pre2 enter u0:0",
    "u1:0 pre4 wo:0 pre6",
    "d2:0 look pre1 d1:0",
    "pre3 d3:0 u0:1 wo:1",
    "u1:1 d0:0 pre5 pre7",
    "wo:2 turns summary d2:1",
    "d1:1 d3:1 near20 u0:2",
    "near21 near10 u1:2 d0:1",
    "near11 wo:3 memory near30",
    "near31 d2:2 near01 d1:2",
    "d3:2 u0:3 u1:3 bank_b",
    "near00 d0:2 d2:3 d1:3",
    "d3:3 bank_c far200 far210",
    "far100 far110 u0:4 far300",
    "far310 far010 far000 far201",
    "far211 far101 far111 far301",
    "far311 far011 far001 u1:4",
    "d0:3 d2:4 d1:4 mix0",
    "d3:4 norm0 up000 up010",
    "u0:5 up020 up030 up100",
    "up110 d0:4 u1:5 up120",
    "up130 d2:5 down20 d1:5",
    "down10 d3:5 down30 d0:5",
    "down00 mix1 norm1 up001",
    "up011 up021 up031 up101",
    "up111 up121 up131 down21",
    "down11 down31 down01",
)


def dot(a, b):
    return jnp.dot(a, b, preferred_element_type=F32)


def normalize(x, gain):
    mean = jnp.sum(x, -1, keepdims=True) * (1.0 / D)
    square = jnp.sum(x * x, -1, keepdims=True) * (1.0 / D)
    return (x - mean) * lax.rsqrt(square - mean * mean + EPS) * gain


def kernel(
    valid, g1, g2, frames, wq, wk, wv, wo, up, dn, out,
    xs, nrm, wqkv, sums, qb, kb, vb, kt, look_out, look_in, so_all, bank, memf, bk, bv,
    wo_b, up_b, dn_b, acc, mx, fo_out, fo_in, mixed, n2, hid, ob,
    loc_sem, send_sem, recv_sem,
):
    tm = lax.axis_index("tm")
    mp = lax.axis_index("mp")
    x = tm // 8
    y = (tm // 2) % 4
    zl = mp // 2
    z = (tm % 2) * 4 + zl
    c = mp % 2
    valid_at = lambda which: valid[which] - tm * SPAN

    def dev(px, py, pz, pc):
        return ((px * 4 + py) * 2 + pz // 4, (pz % 4) * 2 + pc)

    def z_dev(step):
        return dev(x, y, (z + step + 8) % 8, c)

    sibling = (tm, zl * 2 + 1 - c)

    barrier = pltpu.get_barrier_semaphore()

    before, after = ((tm + 31) % 32, mp), ((tm + 1) % 32, mp)
    greeted = [before, after] + [z_dev(step) for step in (1, -1, 2, -2)]
    greeted += [(tm, (mp + i) % 8) for i in range(1, 8)]
    bank_one = [dev((x + i) % 4, y, (z + j) % 8, c) for j in (4, 0) for i in (2, 1, 3, 0) if i or j]
    bank_two = [dev(x, (y + i) % 4, z, c) for i in (2, 1, 3)]
    greeted += bank_one + bank_two
    for other in greeted:
        pl.semaphore_signal(barrier, inc=1, device_id=other, device_id_type=MESH)

    used = [0]
    sent = []

    def remote(src, dst, to):
        i = used[0]
        used[0] += 1
        copy = pltpu.make_async_remote_copy(
            src_ref=src, dst_ref=dst, send_sem=send_sem.at[i], recv_sem=recv_sem.at[i],
            device_id=to, device_id_type=MESH,
        )
        sent.append(copy)
        copy.start()
        return copy

    n_local = [0]

    def local(src, dst):
        i = n_local[0]
        n_local[0] += 1
        copy = pltpu.make_async_copy(src, dst, loc_sem.at[i])
        copy.start()
        return copy

    xs_copies = [local(frames.at[b], xs.at[b]) for b in range(4)]
    w_copies = [
        local(ref, wqkv.at[:, pl.ds(i * 128, 128)]) for i, ref in enumerate((wq, wk, wv))
    ]
    own_copies = [local(wo, wo_b.at[0, 0])]
    for j in range(2):
        own_copies.append(local(up.at[:, pl.ds(j * 256, 256)], up_b.at[j, 0, 0]))

    def q_cols(step):
        return pl.ds(pl.multiple_of(((zl + step) % 4) * 256, 256), 256)

    for r in range(4):
        own_copies.append(local(dn.at[:, q_cols(r)], dn_b.at[r, 0, 0]))

    lx = (x + c) % 4
    ly = (y + c) % 4

    def at_x(label):
        return dev((label + 4 - c) % 4, y, z, c)

    def at_y(label):
        return dev(x, (label + 4 - c) % 4, z, c)

    def first(label):
        return label + 1 - 2 * (label % 2)

    def second(label):
        return 3 - label

    class Half:
        def __init__(self, kind, source, view, base, rows):
            self.source, self.view, self.base, self.rows = source, view, base, rows
            if kind == 0:
                self.a, self.b, self.at_a, self.at_b = lx, ly, at_x, at_y
            else:
                self.a, self.b, self.at_a, self.at_b = ly, lx, at_y, at_x
            self.far = 2 if kind == 0 else -2

        def span(self, index, count):
            return pl.ds(pl.multiple_of(self.base + index * self.rows, self.rows), count * self.rows)

        def z(self):
            here = self.span(self.b * 4 + self.a, 1)
            self.arrive = [
                remote(self.source(1, here), self.view(0, pl.ds(3, 1), here), z_dev(1)),
                remote(self.source(-1, here), self.view(0, pl.ds(1, 1), here), z_dev(-1)),
                remote(self.source(self.far, here), self.view(0, pl.ds(2, 1), here), z_dev(self.far)),
            ]

        def hop(self, rows, to):
            for copy in self.arrive:
                copy.wait_recv()
            part = self.view(0, pl.ds(1, 3), rows)
            self.arrive = [remote(part, part, to)]

        def s1(self):
            for copy in self.arrive:
                copy.wait_recv()
            part = self.view(0, pl.ds(1, 3), self.span(self.b * 4 + self.a, 1))
            self.arrive = [remote(part, part, self.at_a((self.a + i) % 4)) for i in (2, 1, 3)]

        def s2(self):
            self.hop(self.span(self.b * 4, 4), self.at_b(first(self.b)))

        def s3(self):
            near = self.span(8 * (self.b // 2), 8)
            self.hop(near, self.at_b(second(self.b)))
            self.share = [
                remote(self.view(0, pl.ds(1, 3), near), self.view(1, pl.ds(1, 3), near), sibling)
            ]

        def s4(self):
            for copy in self.arrive:
                copy.wait_recv()
            rest = self.span(8 - 8 * (self.b // 2), 8)
            self.share.append(
                remote(self.view(0, pl.ds(1, 3), rest), self.view(1, pl.ds(1, 3), rest), sibling)
            )

        def s5(self):
            for copy in self.share:
                copy.wait_recv()

    class Group:
        def __init__(self, halves, own, own_src):
            self.halves = halves
            self.own, self.own_src = own, own_src

        def z(self):
            for half in self.halves:
                half.z()
            self.own_copies = [
                remote(src, dst.at[pl.ds(1, 1), pl.ds(0, 1)], sibling)
                for src, dst in zip(self.own_src, self.own)
            ]

        def run(self, stage):
            if stage == 0:
                return self.z()
            for half in self.halves:
                getattr(half, "s%d" % stage)()
            if stage == 5:
                for copy in self.own_copies:
                    copy.wait_recv()

    def four(ref, rows, columns):
        return ref.reshape(1, 1, rows, columns)

    def half_up(kind, j):
        return Half(
            kind,
            lambda step, rows: four(up, D, 512).at[0, :, rows, pl.ds(j * 256, 256)],
            lambda e, d, rows: up_b.at[j, e, d, rows, :],
            kind * 512, 32,
        )

    def half_dn(kind, r):
        return Half(
            kind,
            lambda step, rows: four(dn, 512, D).at[0, :, rows, q_cols(r + step + 4)],
            lambda e, d, rows: dn_b.at[r, e, d, rows, :],
            kind * 256, 16,
        )

    groups = {}
    for j in range(2):
        groups["u%d" % j] = Group(
            [half_up(0, j), half_up(1, j)], [up_b.at[j]],
            [four(up, D, 512).at[:, :, :, pl.ds(j * 256, 256)]],
        )
    for r in range(4):
        groups["d%d" % r] = Group(
            [half_dn(0, r), half_dn(1, r)], [dn_b.at[r]],
            [four(dn, 512, D).at[:, :, :, q_cols(r)]],
        )

    class Ring:
        def __init__(self, ref, buf, rows):
            self.ref, self.buf, self.rows = ref, buf, rows

        def run(self, stage):
            buf, half = self.buf, self.rows // 2
            if stage == 0:
                self.up = remote(self.ref, buf.at[0, 3], z_dev(1))
                self.down = remote(self.ref, buf.at[0, 1], z_dev(-1))
                self.share = [remote(self.ref, buf.at[1, 0], sibling)]
            elif stage == 1:
                self.up.wait_recv()
                self.down.wait_recv()
                high, low = pl.ds(half, half), pl.ds(0, half)
                self.far = [
                    remote(buf.at[0, 3, high], buf.at[0, 2, high], z_dev(1)),
                    remote(buf.at[0, 1, low], buf.at[0, 2, low], z_dev(-1)),
                ]
                self.share.append(remote(buf.at[0, 1], buf.at[1, 1], sibling))
                self.share.append(remote(buf.at[0, 3], buf.at[1, 3], sibling))
            elif stage == 2:
                for copy in self.far:
                    copy.wait_recv()
                self.share.append(remote(buf.at[0, 2], buf.at[1, 2], sibling))
            else:
                for copy in self.share:
                    copy.wait_recv()

    groups["wo"] = Ring(wo, wo_b, 128)

    acts = {}

    def action(f):
        acts[f.__name__] = f
        return f

    def loop(f, lo, hi, unroll=1):
        lax.fori_loop(lo, hi, lambda i, carry: (f(i), carry)[1], 0, unroll=unroll)

    @action
    def enter():
        pl.semaphore_wait(barrier, len(greeted))

    held = {}

    def pre(n):
        b, half = n // 2, n % 2
        if n == 0:
            for copy in w_copies:
                copy.wait()
        if half == 0:
            xs_copies[b].wait()

        def norm_rows(i):
            rows = pl.ds(pl.multiple_of(half * OWN + i * 32, 32), 32)
            here = pl.ds(pl.multiple_of(i * 32, 32), 32)
            nrm[n % 2, here, :] = normalize(xs[b, rows, :].astype(F32), g1[...]).astype(BF16)

        loop(norm_rows, 0, 10, unroll=2)
        normed = nrm[n % 2]
        got = dot(normed, wqkv[...])
        rows = slice(half * OWN, half * OWN + OWN)
        qb[b, rows] = got[:, :128].astype(BF16) * jnp.asarray(0.125, BF16)
        kb[b, rows] = got[:, 128:256]
        vb[b, rows] = got[:, 256:].astype(BF16)
        if half == 0:
            look_out[b] = got[:LOOK, 128:].astype(BF16)
        row_i = lax.broadcasted_iota(jnp.int32, (16, OWN), 0)
        col_i = lax.broadcasted_iota(jnp.int32, (16, OWN), 1)
        live = col_i < valid_at(b) - half * OWN
        inside = (col_i >= row_i * SEG) & (col_i < row_i * SEG + SEG) & live
        picks = jnp.where(inside, 1.0, 0.0)
        counts = jnp.sum(picks, -1, keepdims=True)
        total = dot(picks.astype(BF16), normed) / jnp.maximum(counts, 1.0)
        sums[2 * n : 2 * n + 2, :] = total[:2]

    for n in range(8):
        acts["pre%d" % n] = lambda n=n: pre(n)

    @action
    def look():
        held["look"] = remote(look_out, look_in, before)

    def turn(b):
        for sl in range(4):
            kt[b * 4 + sl] = kb[b, sl * SEG : sl * SEG + KEYS].T.astype(BF16)

    @action
    def turns():
        held["look"].wait_recv()
        for b in range(4):
            kb[b, SPAN:] = look_in[b, :, :128].astype(F32)
            vb[b, SPAN:] = look_in[b, :, 128:]
        for copy in own_copies:
            copy.wait()
        loop(turn, 0, 4)

    @action
    def summary():
        asked = dot(sums[...].astype(BF16), wqkv[:, :128]).astype(BF16).astype(F32) * 0.125
        row = lax.broadcasted_iota(jnp.int32, (8, 128), 0)
        head = lax.broadcasted_iota(jnp.int32, (8, 128), 1) // 64
        key_l = lax.broadcasted_iota(jnp.int32, (8, KEYS), 1)
        parts = []
        for g in range(16):
            q = jnp.where(row == head, jnp.broadcast_to(asked[g : g + 1], (8, 128)), 0.0)
            score = dot(q.astype(BF16), kt[g])
            parts.append(jnp.where(key_l < valid_at(g // 4) - (g % 4) * SEG, score, NEG))
        scores = jnp.concatenate(parts, axis=0)
        p = jnp.exp(scores - jnp.max(scores, -1, keepdims=True))
        p = p / jnp.sum(p, -1, keepdims=True)
        parts = []
        for g in range(16):
            at = (g % 4) * SEG
            got = dot(p[g * 8 : g * 8 + 8].astype(BF16), vb[g // 4, at : at + KEYS, :])
            parts.append(jnp.where(head[:1] == 0, got[0:1], got[1:2]))
        so_all[0, 0] = jnp.concatenate(parts, axis=0).astype(BF16)
        held["so"] = []
        for dz in (2, 3, 1, 0):
            for e in range(2):
                if dz or e:
                    to = (tm, ((zl + dz) % 4) * 2 + (c if e == 0 else 1 - c))
                    held["so"].append(remote(so_all.at[0, 0], so_all.at[e, (4 - dz) % 4], to))

    zh = tm % 2

    @action
    def memory():
        for copy in held["so"]:
            copy.wait_recv()
        summed = jnp.concatenate([so_all[e, d] for e in range(2) for d in range(4)], axis=1)
        got = dot(summed, wo_b[...].reshape(D, D)).astype(BF16)
        bank[x, y, zh] = dot(got, wqkv[:, 128:]).astype(BF16)
        part = bank.at[x, y, zh]
        held["bank"] = [remote(part, part, other) for other in bank_one]

    @action
    def bank_b():
        for copy in held["bank"]:
            copy.wait_recv()
        part = bank.at[:, pl.ds(y, 1)]
        held["bank"] = [remote(part, part, other) for other in bank_two]

    @action
    def bank_c():
        for copy in held["bank"]:
            copy.wait_recv()
        memf[0] = bank[:, :, :, :, :128].reshape(SLOTS * 4, 128).astype(F32)
        memf[1] = bank[:, :, :, :, 128:].reshape(SLOTS * 4, 128).astype(F32)
        for b in range(4):
            both = [
                jnp.concatenate(
                    [memf[i, pl.ds(b * 4 + sl, 32, stride=16), :] for sl in range(4)], axis=0
                )
                for i in range(2)
            ]
            bk[b] = both[0].T.astype(BF16)
            bv[b] = both[1].astype(BF16)

    lane = lax.broadcasted_iota(jnp.int32, (SEG, 128), 1)

    def one_head(b, seg, h):
        q = qb[b, pl.ds(pl.multiple_of(seg * SEG, 32), SEG), :]
        mine = lane < 64 if h == 0 else lane >= 64
        return jnp.where(mine, q, jnp.zeros_like(q))

    def with_ones(v):
        return jnp.concatenate([v, jnp.ones_like(v)], axis=1)

    def near_step(b, seg):
        g = b * 4 + seg
        near_l = lax.broadcasted_iota(jnp.int32, (SEG, KEYS), 1)
        ones = with_ones(vb[b, pl.ds(pl.multiple_of(seg * SEG, 32), KEYS), :])
        for h in range(2):
            near = dot(one_head(b, seg, h), kt[g])
            near = jnp.where(near_l < valid_at(b) - seg * SEG, near, NEG)
            top = jnp.max(near, -1, keepdims=True)
            near = jnp.exp(near - top).astype(BF16)
            rows = slice(h * SEG, h * SEG + SEG)
            acc[g, rows] = dot(near, ones)
            mx[g, rows] = jnp.broadcast_to(top, (SEG, 128))

    def far_step(b, seg, dest):
        g = b * 4 + seg
        far_l = lax.broadcasted_iota(jnp.int32, (SEG, SLOTS), 1)
        far_l = (far_l % 32) * 4 + far_l // 32
        far_ok = (far_l < tm * 4 + seg) & (far_l * SEG < valid[b])
        both = []
        for h in range(2):
            rows = slice(h * SEG, h * SEG + SEG)
            far = jnp.where(far_ok, dot(one_head(b, seg, h), bk[b]), NEG)
            before = mx[g, rows]
            top = jnp.maximum(before, jnp.max(far, -1, keepdims=True))
            far = jnp.exp(far - top).astype(BF16)
            keep = jnp.exp(before - top)
            got = dot(far, with_ones(bv[b]))
            total = acc[g, rows, 128:] * keep + got[:, 128:]
            both.append((acc[g, rows, :128] * keep + got[:, :128]) / total)
        dest[...] = jnp.where(lane < 64, both[0], both[1]).astype(BF16)

    def place(r, i):
        return (zl + r) % 4, (c if i == 0 else 1 - c)

    def near(r, i):
        b, core = place(r, i)
        for s in range(2):
            near_step(b, core * 2 + s)

    held["fo"] = [[], []]

    def far(r, i, s):
        b, core = place(r, i)
        rows = pl.ds(s * SEG, SEG)
        if r or i:
            dest = fo_out.at[r, i, rows]
            far_step(b, core * 2 + s, dest)
            there = fo_in.at[i, (4 - r) % 4, rows]
            held["fo"][s].append(remote(dest, there, (tm, b * 2 + core)))
        else:
            far_step(b, core * 2 + s, fo_in.at[0, 0, rows])

    for r in range(4):
        for i in range(2):
            acts["near%d%d" % (r, i)] = lambda r=r, i=i: near(r, i)
            for s in range(2):
                acts["far%d%d%d" % (r, i, s)] = lambda r=r, i=i, s=s: far(r, i, s)

    def mix(s):
        for copy in held["fo"][s]:
            copy.wait_recv()
        part = slice(s * SEG, s * SEG + SEG)
        rows = jnp.concatenate([fo_in[e, d, part] for e in range(2) for d in range(4)], axis=1)
        own = pl.ds(pl.multiple_of(c * OWN + s * SEG, 32), SEG)
        for n in range(4):
            weight = wo_b[:, :, :, n * 256 : n * 256 + 256].reshape(D, 256)
            mixed[n, part] = dot(rows, weight) + xs[zl, own, n * 256 : n * 256 + 256].astype(F32)

    def norm_two(s):
        def step(i):
            rows = pl.ds(pl.multiple_of(s * SEG + i * 32, 32), 32)
            v = jnp.concatenate([mixed[n, rows, :] for n in range(4)], axis=1)
            n2[rows, :] = normalize(v, g2[...]).astype(BF16)

        loop(step, 0, 5)

    def up_step(j, b, s):
        part = slice(s * SEG, s * SEG + SEG)
        h = dot(n2[part, :], up_b[j, b // 4, b % 4])
        h = 0.5 * h * (1.0 + lax.erf(h * (2.0 ** -0.5)))
        hid[part, pl.ds(pl.multiple_of(b * 512 + j * 256, 256), 256)] = h.astype(BF16)

    for s in range(2):
        acts["mix%d" % s] = lambda s=s: mix(s)
        acts["norm%d" % s] = lambda s=s: norm_two(s)
        for j in range(2):
            for k in range(4):
                acts["up%d%d%d" % (j, k, s)] = lambda j=j, k=k, s=s: loop(
                    lambda b: up_step(j, b, s), 2 * k, 2 * k + 2, unroll=2)

    outs = []
    held["home"] = []

    def down(r, s):
        part = slice(s * SEG, s * SEG + SEG)
        rows = pl.ds(s * SEG, SEG)
        there = out.at[zl, pl.ds(pl.multiple_of(c * OWN + s * SEG, 32), SEG), :]
        block = dot(hid[part, :], dn_b[r].reshape(4 * D, 256))
        to = (zl + r) % 4
        block = (block + mixed[to, part]).astype(BF16)
        ob[r, 0, part] = block[:, :128]
        ob[r, 1, part] = block[:, 128:]
        if r:
            for core in (c, 1 - c):
                outs.append(remote(ob.at[r, core, rows], there, (tm, to * 2 + core)))
        else:
            outs.append(remote(ob.at[0, 1 - c, rows], there, sibling))
            held["home"].append(local(ob.at[0, c, rows], there))

    for r in range(4):
        for s in range(2):
            acts["down%d%d" % (r, s)] = lambda r=r, s=s: down(r, s)

    for token in " ".join(SCHEDULE).split():
        if ":" in token:
            name, stage = token.split(":")
            groups[name].run(int(stage))
        else:
            acts[token]()
    for copy in held["home"]:
        copy.wait()
    for copy in outs:
        copy.wait_recv()
    for copy in sent:
        copy.wait_send()
    assert used[0] <= N_SEM, used[0]


def body(frames, valid, ln1_gain, w_query, w_key, w_value, w_out, ln2_gain, w_up, w_down):
    vmem = pl.BlockSpec(memory_space=pltpu.VMEM)
    anywhere = pl.BlockSpec(memory_space=pl.ANY)
    scratch = [
        pltpu.VMEM((4, SPAN, D), BF16),
        pltpu.VMEM((2, OWN, D), BF16),
        pltpu.VMEM((D, 384), BF16),
        pltpu.VMEM((16, D), F32),
        pltpu.VMEM((4, SPAN, 128), BF16),
        pltpu.VMEM((4, SPAN + LOOK, 128), F32),
        pltpu.VMEM((4, SPAN + LOOK, 128), BF16),
        pltpu.VMEM((16, 128, KEYS), BF16),
        pltpu.VMEM((4, LOOK, 256), BF16),
        pltpu.VMEM((4, LOOK, 256), BF16),
        pltpu.VMEM((2, 4, 16, 128), BF16),
        pltpu.VMEM((4, 4, 2, 16, 256), BF16),
        pltpu.VMEM((2, SLOTS * 4, 128), F32),
        pltpu.VMEM((4, 128, SLOTS), BF16),
        pltpu.VMEM((4, SLOTS, 128), BF16),
        pltpu.VMEM((2, 4, 128, D), BF16),
        pltpu.VMEM((2, 2, 4, D, 256), BF16),
        pltpu.VMEM((4, 2, 4, 512, 256), BF16),
        pltpu.VMEM((16, OWN, 256), F32),
        pltpu.VMEM((16, OWN, 128), F32),
        pltpu.VMEM((4, 2, OWN, 128), BF16),
        pltpu.VMEM((2, 4, OWN, 128), BF16),
        pltpu.VMEM((4, OWN, 256), F32),
        pltpu.VMEM((OWN, D), BF16),
        pltpu.VMEM((OWN, 4 * D), BF16),
        pltpu.VMEM((4, 2, OWN, 128), BF16),
        pltpu.SemaphoreType.DMA((16,)),
        pltpu.SemaphoreType.DMA((N_SEM,)),
        pltpu.SemaphoreType.DMA((N_SEM,)),
    ]
    return pl.pallas_call(
        kernel,
        name="layer",
        out_shape=jax.ShapeDtypeStruct((frames.shape[0], frames.shape[1], 128), BF16),
        in_specs=[pl.BlockSpec(memory_space=pltpu.SMEM), vmem, vmem] + [anywhere] * 7,
        out_specs=anywhere,
        scratch_shapes=scratch,
        compiler_params=pltpu.CompilerParams(
            collective_id=0, has_side_effects=True, vmem_limit_bytes=56 * 2**20
        ),
    )(
        valid, ln1_gain.reshape(1, D), ln2_gain.reshape(1, D),
        frames, w_query, w_key, w_value, w_out, w_up, w_down,
    )


def solution(mesh):
    placed = (
        P(None, "tm", None),
        P(),
        P(),
        P(None, "mp"),
        P(None, "mp"),
        P(None, "mp"),
        P("mp", None),
        P(),
        P(None, "mp"),
        P("mp", None),
    )
    return jax.shard_map(
        body, mesh=mesh, in_specs=placed, out_specs=P(None, "tm", "mp"), check_vma=False
    )
```
